512 devices in a mesh: row: 32 (over y, x_lo, core), col: 16 (over x_hi, z).
Axes of the slice: x: 4 (x_hi: 2, x_lo: 2; x = x_hi * 2 + x_lo), y: 8, z: 8, core: 2. Of those that a mesh axis runs over, the one named last changes fastest.
Arguments:
- cotangent: bfloat16 [196608, 128], P(('row', 'col')), may hold values from -6 to 6
- pre_act: bfloat16 [196608, 128], P(('row', 'col')), may hold values from -6 to 6
- aggregated: bfloat16 [196608, 128], P(('row', 'col')), may hold values from -6 to 6
- weight: bfloat16 [128, 128], replicated, may hold values from -0.5 to 0.5
- tile_values: bfloat16 [16384, 128, 128], P(('row', 'col')), may hold values from -0.15625 to 0.15625
- tile_in: int32 [16384], P(('row', 'col')), may hold values from 0 to 1535, as said below
- tile_out: int32 [16384], P(('row', 'col')), may hold values from 0 to 1535, as said below
- order: int32 [196608], P(('row', 'col')), may hold values from 0 to 196607, as said below
Outputs:
- node_grad: bfloat16 [196608, 128], P(('row', 'col'))
- weight_grad: float32 [128, 128], replicated
The draws below stay inside these ranges and needn't reach their ends.
Inputs may be any that keep to these rules, and one draw needn't show every extreme that they name: `tile_in`: devices are numbered row-major over (row, col), each holding 32 tiles and 3 consecutive blocks. A tile of the device at (r, c) reads a block held by the device (r + d mod 32, c) with -8 <= d <= 8; on every device one tile has d = -8 and one d = 8. `tile_out`: A tile of the device at (r, c) writes a block held by some device of row r. `order`: maps the rows of each device onto the rows of the same device, each once.
All inputs are finite; a program needn't handle non-finite values.
Results may differ from the reference program's by a relative error of at most 0.0049.
Values may be sent and summed in bfloat16 or wider, within the bound.
No kernel may reach another device: no remote copies, remote signals or barrier semaphores. Data moves between devices by JAX's collectives and lax.ppermute only.
A program may use at most 64 MiB of HBM per device.

```python
import math
import jax
import jax.numpy as jnp
from jax import lax

F = 128
BLK = 128
NB_DEV = 3
TILES = 32
REACH = 8
NODES = 196608
N_ROW = 32
N_COL = 16
DEVICES = 512


def draw_tile_out(key, part):
    key = jax.random.fold_in(key, 11)
    first, second = jax.random.split(key)
    device = jnp.arange(DEVICES * TILES, dtype=jnp.int32) // TILES
    group = device // N_COL
    column = jax.random.randint(first, (DEVICES * TILES,), 0, N_COL, dtype=jnp.int32)
    local = jax.random.randint(second, (DEVICES * TILES,), 0, NB_DEV, dtype=jnp.int32)
    return ((group * N_COL + column) * NB_DEV + local).astype(jnp.int32)


def draw_tile_in(key, part):
    key = jax.random.fold_in(key, 23)
    first, second = jax.random.split(key)
    flat = jnp.arange(DEVICES * TILES, dtype=jnp.int32)
    device = flat // TILES
    within = flat % TILES
    group = device // N_COL
    column = device % N_COL
    distance = jax.random.randint(first, (DEVICES * TILES,), -REACH, REACH + 1, dtype=jnp.int32)
    distance = jnp.where(within == 0, -REACH, jnp.where(within == 1, REACH, distance))
    source_group = (group + distance) % N_ROW
    local = jax.random.randint(second, (DEVICES * TILES,), 0, NB_DEV, dtype=jnp.int32)
    return ((source_group * N_COL + column) * NB_DEV + local).astype(jnp.int32)


def draw_order(key, part):
    key = jax.random.fold_in(key, 37)
    keys = jax.random.split(key, DEVICES)
    rows_dev = NB_DEV * BLK
    shuffled = jax.vmap(lambda single: jax.random.permutation(single, rows_dev))(keys).astype(jnp.int32)
    offsets = (jnp.arange(DEVICES, dtype=jnp.int32) * rows_dev)[:, None]
    return (shuffled + offsets).reshape(-1).astype(jnp.int32)


def level_of(stream_key, extent, shards, low, largest):
    level = 1.0
    for position, shards_of in shards:
        draws = jax.random.uniform(jax.random.fold_in(jax.random.fold_in(stream_key, 6), position), (shards_of,), jnp.float32, low / len(shards), largest / len(shards))
        level = level * jnp.repeat(jnp.exp(draws), extent[position] // shards_of).reshape((-1,) + (1,) * (len(extent) - 1 - position))
    return level


def bell_draw(rng, shape, width, most, cuts=(), kind=jnp.bfloat16):
    loudness = level_of(rng, shape, cuts, -0.22, 0.18) if cuts else 1.0
    values = jax.random.normal(rng, shape, jnp.float32) * width * loudness
    return jnp.minimum(jnp.maximum(values, -most), most).astype(kind)


def setup_inputs(seed: int = 0) -> dict:
    key_of = jax.random.split(jax.random.key(seed), 9)
    cotangent = bell_draw(key_of[0], (NODES, F), 1.0, 6.0, ((0, 512),))
    pre_act = bell_draw(key_of[1], (NODES, F), 1.0, 6.0, ((0, 512),))
    aggregated = bell_draw(key_of[2], (NODES, F), 1.0, 6.0, ((0, 512),))
    weight = bell_draw(key_of[3], (F, F), F ** -0.5, 0.5)
    tile_values = bell_draw(key_of[4], (DEVICES * TILES, BLK, BLK), (TILES * BLK // NB_DEV) ** -0.5, 0.15625, ((0, 512),))
    tile_in = draw_tile_in(jax.random.fold_in(key_of[8], 71), 0)
    tile_out = draw_tile_out(jax.random.fold_in(key_of[8], 71), 0)
    order = draw_order(jax.random.fold_in(key_of[8], 71), 0)
    return dict(cotangent=cotangent, pre_act=pre_act, aggregated=aggregated, weight=weight, tile_values=tile_values, tile_in=tile_in, tile_out=tile_out, order=order)


def reference(cotangent, pre_act, aggregated, weight, tile_values, tile_in, tile_out, order):
    grad_rows = jnp.take(cotangent, order, axis=0)
    grad_pre = jnp.where(pre_act > 0, grad_rows, jnp.zeros_like(grad_rows))
    weight_grad = jnp.dot(aggregated.T, grad_pre, preferred_element_type=jnp.float32) * (1.0 / math.sqrt(NODES))
    grad_agg = jnp.dot(grad_pre, weight.T, preferred_element_type=jnp.float32).astype(jnp.bfloat16)
    blocks = grad_agg.reshape(-1, BLK, F)
    tiles = tile_values.reshape(-1, TILES, BLK, BLK)
    sources = tile_in.reshape(-1, TILES)
    targets = tile_out.reshape(-1, TILES)

    def absorb(total, pack):
        values, source, target = pack
        picked = jnp.take(blocks, source, axis=0).astype(jnp.float32)
        product = jnp.einsum('tij,tjf->tif', values.astype(jnp.float32), picked)
        return (total.at[target].add(product), None)
    total, unused = lax.scan(absorb, jnp.zeros(blocks.shape, jnp.float32), (tiles, sources, targets))
    node_grad = total.reshape(-1, F).astype(jnp.bfloat16)
    return (node_grad, weight_grad)
```

```python
import functools

import jax
import jax.numpy as jnp
from jax import lax
from jax.experimental import pallas as pl
from jax.experimental.pallas import tpu as pltpu
from jax.sharding import PartitionSpec as P

BF = jnp.bfloat16
F32 = jnp.float32
SIDE = 128
PLANE = 4


def dot(a, b, contract):
    return lax.dot_general(a, b, ((contract[:1], contract[1:]), ((), ())), preferred_element_type=F32)


def adjoint_kernel(base_ref, order_ref, cot_ref, pre_ref, agg_ref, w_ref, out_ref, wpart_ref):
    rows = cot_ref.shape[0]
    cot = cot_ref[...]
    row_id = lax.broadcasted_iota(jnp.int32, (rows, SIDE), 0)
    base = base_ref[0]
    total = jnp.zeros(wpart_ref.shape, F32)
    for b in range(rows // SIDE):
        span = slice(b * SIDE, (b + 1) * SIDE)
        local = order_ref[b : b + 1, :] - base
        pick = jnp.where(row_id == local, 1.0, 0.0).astype(BF)
        grad_rows = dot(pick, cot, (0, 0))
        grad_pre = jnp.where(pre_ref[span, :].astype(F32) > 0, grad_rows, 0.0).astype(BF)
        total += dot(agg_ref[span, :], grad_pre, (0, 0))
        out_ref[span, :] = dot(grad_pre, w_ref[...], (1, 1)).astype(BF)
    wpart_ref[...] = total


def tile_kernel(src_ref, dst_ref, tiles_ref, blocks_ref, wsum_ref, out_ref, acc_ref):
    cols, rows, _ = out_ref.shape
    share = wsum_ref.shape[0]
    blocks = (rows - 2 * share) // SIDE
    acc_ref[...] = jnp.zeros_like(acc_ref)

    def one(t, carry):
        at = pl.multiple_of(src_ref[t] * SIDE, SIDE)
        to = dst_ref[t]
        acc_ref[to] += dot(tiles_ref[t], blocks_ref[pl.ds(at, SIDE), :], (1, 0))
        return carry

    lax.fori_loop(0, tiles_ref.shape[0], one, 0, unroll=8)
    high = wsum_ref[...].astype(BF)
    low = (wsum_ref[...] - high.astype(F32)).astype(BF)
    both = jnp.concatenate([high, low], axis=0)
    for c in range(cols):
        for b in range(blocks):
            out_ref[c, b * SIDE : (b + 1) * SIDE, :] = acc_ref[c * blocks + b].astype(BF)
        out_ref[c, blocks * SIDE :, :] = both


def finish_kernel(scale, got_ref, out_ref, wgrad_ref):
    cols, rows, _ = got_ref.shape
    share = wgrad_ref.shape[0] // cols
    nodes = rows - 2 * share
    total = got_ref[0, :nodes, :].astype(F32)
    for c in range(1, cols):
        total += got_ref[c, :nodes, :].astype(F32)
    out_ref[...] = total.astype(BF)
    for c in range(cols):
        pair = got_ref[c, nodes:, :].astype(F32)
        wgrad_ref[c * share : (c + 1) * share, :] = (pair[:share] + pair[share:]) * scale


def vmem():
    return pl.BlockSpec(memory_space=pltpu.VMEM)


def smem():
    return pl.BlockSpec(memory_space=pltpu.SMEM)


def on_device(cotangent, pre_act, aggregated, weight, tile_values, tile_in, tile_out, order):
    row_count = lax.axis_size("row")
    col_count = lax.axis_size("col")
    row_pos = lax.axis_index("row")
    col_pos = lax.axis_index("col")
    nodes, feat = cotangent.shape
    blocks_dev = nodes // SIDE
    planes = row_count // PLANE
    params = pltpu.CompilerParams(vmem_limit_bytes=24 << 20)

    base = ((row_pos * col_count + col_pos) * nodes).astype(jnp.int32).reshape(1)
    adjoint, wpart = pl.pallas_call(
        adjoint_kernel,
        out_shape=(jax.ShapeDtypeStruct((nodes, feat), BF), jax.ShapeDtypeStruct((feat, feat), F32)),
        in_specs=[smem()] + [vmem()] * 5,
        out_specs=(vmem(), vmem()),
        compiler_params=params,
        name="adjoint",
    )(base, order.reshape(blocks_dev, SIDE), cotangent, pre_act, aggregated, weight)

    def swap(value, bit):
        return lax.ppermute(value, "row", [(i, i ^ bit) for i in range(row_count)])

    def to_plane(value, steps):
        pairs = [(i, (i + PLANE * (steps if i % 2 == 0 else -steps)) % row_count) for i in range(row_count)]
        return lax.ppermute(value, "row", pairs)

    chip = jnp.concatenate([adjoint, swap(adjoint, 1)])
    near = to_plane(chip, 1)
    far = to_plane(chip, 2)
    mine = jnp.concatenate([near, far])
    side = swap(jnp.concatenate([adjoint, mine]), 2)
    half = jnp.concatenate([mine, side])
    other = swap(half, 1)
    sources = jnp.concatenate([chip, half, other])

    share = feat // col_count
    chunk = lax.all_to_all(wpart.reshape(col_count, share, feat), "col", 0, 0).sum(0)
    wsum = lax.all_to_all(jnp.broadcast_to(chunk, (row_count, share, feat)), "row", 0, 0).sum(0)

    source_device = tile_in // blocks_dev
    group = source_device // col_count
    local = tile_in % blocks_dev
    plane_gap = (group // PLANE - row_pos // PLANE) % planes
    other_chip = ((group // 2) ^ (row_pos // 2)) & 1
    other_core = (group ^ row_pos) & 1
    core = row_pos & 1
    below = plane_gap > planes // 2
    steps = jnp.where(below, planes - plane_gap, plane_gap)
    holder = jnp.where(below, 0, 1)
    from_core = group & 1
    sent_by_other = from_core ^ holder
    in_half = jnp.where(
        other_chip == 0,
        (steps - 1) * 2 + sent_by_other,
        4 + jnp.where(plane_gap == 0, 0, 1 + (steps - 1) * 2 + sent_by_other),
    )
    half_slots = 9
    holder = jnp.where(plane_gap == 0, from_core, holder)
    slot = 2 + in_half + jnp.where(holder == core, 0, half_slots)
    slot = jnp.where((plane_gap == 0) & (other_chip == 0), other_core, slot)
    src_index = slot * blocks_dev + local
    dst_index = tile_out - row_pos * col_count * blocks_dev

    rows_out = nodes + 2 * share
    tiles = tile_values.shape[0]
    sends = pl.pallas_call(
        tile_kernel,
        out_shape=jax.ShapeDtypeStruct((col_count, rows_out, feat), BF),
        in_specs=[smem(), smem(), vmem(), vmem(), vmem()],
        out_specs=vmem(),
        scratch_shapes=[pltpu.VMEM((col_count * blocks_dev, SIDE, feat), F32)],
        compiler_params=params,
        cost_estimate=pl.CostEstimate(
            flops=2 * tiles * SIDE * SIDE * feat, bytes_accessed=6 << 20, transcendentals=0
        ),
        name="tiles",
    )(src_index, dst_index, tile_values, sources, wsum)

    got = lax.all_to_all(sends, "col", 0, 0)
    scale = 1.0 / float(nodes * row_count * col_count) ** 0.5
    node_grad, weight_grad = pl.pallas_call(
        functools.partial(finish_kernel, scale),
        out_shape=(jax.ShapeDtypeStruct((nodes, feat), BF), jax.ShapeDtypeStruct((feat, feat), F32)),
        in_specs=[vmem()],
        out_specs=(vmem(), vmem()),
        compiler_params=params,
        name="finish",
    )(got)
    return (node_grad, weight_grad)


def solution(mesh):
    split = P(("row", "col"))
    return jax.shard_map(
        on_device,
        mesh=mesh,
        in_specs=(split, split, split, P(), split, split, split, split),
        out_specs=(split, P()),
        check_vma=False,
    )
```

```python
import functools

import jax
import jax.numpy as jnp
from jax import lax
from jax.experimental import pallas as pl
from jax.experimental.pallas import tpu as pltpu
from jax.sharding import PartitionSpec as P

BF = jnp.bfloat16
F32 = jnp.float32
SIDE = 128
PLANE = 4


def dot(a, b, contract):
    return lax.dot_general(a, b, ((contract[:1], contract[1:]), ((), ())), preferred_element_type=F32)


def adjoint_kernel(base_ref, order_in, cot_in, pre_in, agg_in, w_in, out_ref, wpart_ref, order_ref, cot_ref, pre_ref, agg_ref, w_ref, sems):
    ins = (order_in, cot_in, pre_in, w_in, agg_in)
    held = (order_ref, cot_ref, pre_ref, w_ref, agg_ref)
    copies = [pltpu.make_async_copy(a, b, sems.at[i]) for i, (a, b) in enumerate(zip(ins, held))]
    for copy in copies:
        copy.start()
    for copy in copies:
        copy.wait()
    rows = cot_ref.shape[0]
    cot = cot_ref[...]
    row_id = lax.broadcasted_iota(jnp.int32, (rows, SIDE), 0)
    base = base_ref[0]
    total = jnp.zeros(wpart_ref.shape, F32)
    for b in range(rows // SIDE):
        span = slice(b * SIDE, (b + 1) * SIDE)
        local = order_ref[b : b + 1, :] - base
        pick = jnp.where(row_id == local, 1.0, 0.0).astype(BF)
        grad_rows = dot(pick, cot, (0, 0))
        grad_pre = jnp.where(pre_ref[span, :].astype(F32) > 0, grad_rows, 0.0).astype(BF)
        total += dot(agg_ref[span, :], grad_pre, (0, 0))
        out_ref[span, :] = dot(grad_pre, w_ref[...], (1, 1)).astype(BF)
    wpart_ref[...] = total


def tile_kernel(src_ref, dst_ref, tiles_ref, own, beside, near, far, side, other_near, other_side, wrow_ref, out_ref, blocks_ref, acc_ref):
    cols, rows, _ = out_ref.shape
    share = wrow_ref.shape[1]
    at = 0
    for piece in (own, beside, near, far, side, other_near, other_side):
        blocks_ref[at : at + piece.shape[0], :] = piece[...]
        at += piece.shape[0]
    blocks = (rows - 2 * share) // SIDE
    acc_ref[...] = jnp.zeros_like(acc_ref)

    def one(t, carry):
        at = pl.multiple_of(src_ref[t] * SIDE, SIDE)
        to = dst_ref[t]
        acc_ref[to] += dot(tiles_ref[t], blocks_ref[pl.ds(at, SIDE), :], (1, 0))
        return carry

    lax.fori_loop(0, tiles_ref.shape[0], one, 0, unroll=8)
    wsum = wrow_ref[0]
    for r in range(1, wrow_ref.shape[0]):
        wsum += wrow_ref[r]
    high = wsum.astype(BF)
    low = (wsum - high.astype(F32)).astype(BF)
    both = jnp.concatenate([high, low], axis=0)
    for c in range(cols):
        for b in range(blocks):
            out_ref[c, b * SIDE : (b + 1) * SIDE, :] = acc_ref[c * blocks + b].astype(BF)
        out_ref[c, blocks * SIDE :, :] = both


def finish_kernel(scale, got_ref, out_ref, wgrad_ref):
    cols, rows, _ = got_ref.shape
    share = wgrad_ref.shape[0] // cols
    nodes = rows - 2 * share
    total = got_ref[0, :nodes, :].astype(F32)
    for c in range(1, cols):
        total += got_ref[c, :nodes, :].astype(F32)
    out_ref[...] = total.astype(BF)
    for c in range(cols):
        pair = got_ref[c, nodes:, :].astype(F32)
        wgrad_ref[c * share : (c + 1) * share, :] = (pair[:share] + pair[share:]) * scale


def vmem():
    return pl.BlockSpec(memory_space=pltpu.VMEM)


def smem():
    return pl.BlockSpec(memory_space=pltpu.SMEM)


def on_device(cotangent, pre_act, aggregated, weight, tile_values, tile_in, tile_out, order):
    row_count = lax.axis_size("row")
    col_count = lax.axis_size("col")
    row_pos = lax.axis_index("row")
    col_pos = lax.axis_index("col")
    nodes, feat = cotangent.shape
    blocks_dev = nodes // SIDE
    planes = row_count // PLANE
    params = pltpu.CompilerParams(vmem_limit_bytes=12 << 20)

    base = ((row_pos * col_count + col_pos) * nodes).astype(jnp.int32).reshape(1)
    adjoint, wpart = pl.pallas_call(
        adjoint_kernel,
        out_shape=(jax.ShapeDtypeStruct((nodes, feat), BF), jax.ShapeDtypeStruct((feat, feat), F32)),
        in_specs=[smem()] + [pl.BlockSpec(memory_space=pltpu.HBM)] * 5,
        out_specs=(vmem(), vmem()),
        scratch_shapes=[
            pltpu.VMEM((blocks_dev, SIDE), jnp.int32),
            pltpu.VMEM((nodes, feat), BF),
            pltpu.VMEM((nodes, feat), BF),
            pltpu.VMEM((nodes, feat), BF),
            pltpu.VMEM((feat, feat), BF),
            pltpu.SemaphoreType.DMA((5,)),
        ],
        compiler_params=pltpu.CompilerParams(vmem_limit_bytes=60 << 20),
        name="adjoint",
    )(base, order.reshape(blocks_dev, SIDE), cotangent, pre_act, aggregated, weight)

    def swap(value, bit):
        return lax.ppermute(value, "row", [(i, i ^ bit) for i in range(row_count)])

    def to_plane(value, steps):
        pairs = [(i, (i + PLANE * (steps if i % 2 == 0 else -steps)) % row_count) for i in range(row_count)]
        return lax.ppermute(value, "row", pairs)

    share = feat // col_count
    chunk = lax.all_to_all(wpart.reshape(col_count, share, feat), "col", 0, 0).sum(0)
    copies = jnp.broadcast_to(chunk, (row_count, share, feat))

    beside = swap(adjoint, 1)
    chip = jnp.concatenate([adjoint, beside])
    near = to_plane(chip, 1)
    far = to_plane(chip, 2)
    across, copies = lax.optimization_barrier((jnp.concatenate([adjoint, near, far]), copies))
    side = swap(across, 2)
    wrow = lax.all_to_all(copies, "row", 0, 0)
    other_near = swap(jnp.concatenate([near, far]), 1)
    side, other_near, wrow = lax.optimization_barrier((side, other_near, wrow))
    other_side = swap(side, 1)

    source_device = tile_in // blocks_dev
    group = source_device // col_count
    local = tile_in % blocks_dev
    plane_gap = (group // PLANE - row_pos // PLANE) % planes
    other_chip = ((group // 2) ^ (row_pos // 2)) & 1
    other_core = (group ^ row_pos) & 1
    core = row_pos & 1
    below = plane_gap > planes // 2
    steps = jnp.where(below, planes - plane_gap, plane_gap)
    holder = jnp.where(below, 0, 1)
    from_core = group & 1
    sent_by_other = from_core ^ holder
    in_half = jnp.where(
        other_chip == 0,
        (steps - 1) * 2 + sent_by_other,
        4 + jnp.where(plane_gap == 0, 0, 1 + (steps - 1) * 2 + sent_by_other),
    )
    half_slots = 9
    holder = jnp.where(plane_gap == 0, from_core, holder)
    slot = 2 + in_half + jnp.where(holder == core, 0, half_slots)
    slot = jnp.where((plane_gap == 0) & (other_chip == 0), other_core, slot)
    src_index = slot * blocks_dev + local
    dst_index = tile_out - row_pos * col_count * blocks_dev

    rows_out = nodes + 2 * share
    tiles = tile_values.shape[0]
    sends = pl.pallas_call(
        tile_kernel,
        out_shape=jax.ShapeDtypeStruct((col_count, rows_out, feat), BF),
        in_specs=[smem(), smem()] + [vmem()] * 9,
        out_specs=vmem(),
        scratch_shapes=[
            pltpu.VMEM((20 * nodes, feat), BF),
            pltpu.VMEM((col_count * blocks_dev, SIDE, feat), F32),
        ],
        compiler_params=params,
        cost_estimate=pl.CostEstimate(
            flops=2 * tiles * SIDE * SIDE * feat, bytes_accessed=6 << 20, transcendentals=0
        ),
        name="tiles",
    )(src_index, dst_index, tile_values, adjoint, beside, near, far, side, other_near, other_side, wrow)

    got = lax.all_to_all(sends, "col", 0, 0)
    scale = 1.0 / float(nodes * row_count * col_count) ** 0.5
    node_grad, weight_grad = pl.pallas_call(
        functools.partial(finish_kernel, scale),
        out_shape=(jax.ShapeDtypeStruct((nodes, feat), BF), jax.ShapeDtypeStruct((feat, feat), F32)),
        in_specs=[vmem()],
        out_specs=(vmem(), vmem()),
        compiler_params=params,
        name="finish",
    )(got)
    return (node_grad, weight_grad)


def solution(mesh):
    split = P(("row", "col"))
    return jax.shard_map(
        on_device,
        mesh=mesh,
        in_specs=(split, split, split, P(), split, split, split, split),
        out_specs=(split, P()),
        check_vma=False,
    )
```

```python
import functools

import jax
import jax.numpy as jnp
from jax import lax
from jax.experimental import pallas as pl
from jax.experimental.pallas import tpu as pltpu
from jax.sharding import PartitionSpec as P

BF = jnp.bfloat16
F32 = jnp.float32
SIDE = 128
PLANE = 4


def dot(a, b, contract):
    return lax.dot_general(a, b, ((contract[:1], contract[1:]), ((), ())), preferred_element_type=F32)


def adjoint_kernel(base_ref, order_in, cot_in, pre_in, agg_in, w_in, out_ref, wpart_ref, order_ref, cot_ref, pre_ref, agg_ref, w_ref, sems):
    ins = (order_in, cot_in, pre_in, w_in, agg_in)
    held = (order_ref, cot_ref, pre_ref, w_ref, agg_ref)
    copies = [pltpu.make_async_copy(a, b, sems.at[i]) for i, (a, b) in enumerate(zip(ins, held))]
    for copy in copies:
        copy.start()
    for copy in copies:
        copy.wait()
    rows = cot_ref.shape[0]
    cot = cot_ref[...]
    row_id = lax.broadcasted_iota(jnp.int32, (rows, SIDE), 0)
    base = base_ref[0]
    total = jnp.zeros(wpart_ref.shape, F32)
    for b in range(rows // SIDE):
        span = slice(b * SIDE, (b + 1) * SIDE)
        local = order_ref[b : b + 1, :] - base
        pick = jnp.where(row_id == local, 1.0, 0.0).astype(BF)
        grad_rows = dot(pick, cot, (0, 0))
        grad_pre = jnp.where(pre_ref[span, :].astype(F32) > 0, grad_rows, 0.0).astype(BF)
        total += dot(agg_ref[span, :], grad_pre, (0, 0))
        out_ref[span, :] = dot(grad_pre, w_ref[...], (1, 1)).astype(BF)
    wpart_ref[...] = total


def tile_kernel(src_ref, dst_ref, tiles_ref, own, beside, near, far, side, other_near, other_side, out_ref, blocks_ref, acc_ref):
    cols, rows, _ = out_ref.shape
    at = 0
    for piece in (own, beside, near, far, side, other_near, other_side):
        blocks_ref[at : at + piece.shape[0], :] = piece[...]
        at += piece.shape[0]
    blocks = rows // SIDE
    acc_ref[...] = jnp.zeros_like(acc_ref)

    def one(t, carry):
        at = pl.multiple_of(src_ref[t] * SIDE, SIDE)
        to = dst_ref[t]
        acc_ref[to] += dot(tiles_ref[t], blocks_ref[pl.ds(at, SIDE), :], (1, 0))
        return carry

    lax.fori_loop(0, tiles_ref.shape[0], one, 0, unroll=8)
    for c in range(cols):
        for b in range(blocks):
            out_ref[c, b * SIDE : (b + 1) * SIDE, :] = acc_ref[c * blocks + b].astype(BF)


def finish_kernel(scale, got_ref, wsum_ref, out_ref, wgrad_ref):
    total = got_ref[0].astype(F32)
    for c in range(1, got_ref.shape[0]):
        total += got_ref[c].astype(F32)
    out_ref[...] = total.astype(BF)
    wgrad_ref[...] = wsum_ref[...] * scale


def vmem():
    return pl.BlockSpec(memory_space=pltpu.VMEM)


def smem():
    return pl.BlockSpec(memory_space=pltpu.SMEM)


def on_device(cotangent, pre_act, aggregated, weight, tile_values, tile_in, tile_out, order):
    row_count = lax.axis_size("row")
    col_count = lax.axis_size("col")
    row_pos = lax.axis_index("row")
    col_pos = lax.axis_index("col")
    nodes, feat = cotangent.shape
    blocks_dev = nodes // SIDE
    planes = row_count // PLANE
    params = pltpu.CompilerParams(vmem_limit_bytes=12 << 20)

    base = ((row_pos * col_count + col_pos) * nodes).astype(jnp.int32).reshape(1)
    adjoint, wpart = pl.pallas_call(
        adjoint_kernel,
        out_shape=(jax.ShapeDtypeStruct((nodes, feat), BF), jax.ShapeDtypeStruct((feat, feat), F32)),
        in_specs=[smem()] + [pl.BlockSpec(memory_space=pltpu.HBM)] * 5,
        out_specs=(vmem(), vmem()),
        scratch_shapes=[
            pltpu.VMEM((blocks_dev, SIDE), jnp.int32),
            pltpu.VMEM((nodes, feat), BF),
            pltpu.VMEM((nodes, feat), BF),
            pltpu.VMEM((nodes, feat), BF),
            pltpu.VMEM((feat, feat), BF),
            pltpu.SemaphoreType.DMA((5,)),
        ],
        compiler_params=pltpu.CompilerParams(vmem_limit_bytes=60 << 20),
        name="adjoint",
    )(base, order.reshape(blocks_dev, SIDE), cotangent, pre_act, aggregated, weight)

    def swap(value, bit):
        return lax.ppermute(value, "row", [(i, i ^ bit) for i in range(row_count)])

    def to_plane(value, steps):
        pairs = [(i, (i + PLANE * (steps if i % 2 == 0 else -steps)) % row_count) for i in range(row_count)]
        return lax.ppermute(value, "row", pairs)

    def with_partner(value, axis, bit):
        pairs = [(i, i ^ bit) for i in range(lax.axis_size(axis))]
        return value + lax.ppermute(value, axis, pairs)

    beside = swap(adjoint, 1)
    chip = jnp.concatenate([adjoint, beside])
    near = to_plane(chip, 1)
    far = to_plane(chip, 2)
    col_bits = [1 << k for k in reversed(range((col_count - 1).bit_length()))]
    row_bits = [1 << k for k in range((row_count - 1).bit_length())]
    wsum = wpart
    for bit in col_bits[:1]:
        wsum = with_partner(wsum, "col", bit)
    across, wsum = lax.optimization_barrier((jnp.concatenate([adjoint, near, far]), wsum))
    side = swap(across, 2)
    other_near = swap(jnp.concatenate([near, far]), 1)
    for bit in col_bits[1:2]:
        wsum = with_partner(wsum, "col", bit)
    side, other_near, wsum = lax.optimization_barrier((side, other_near, wsum))
    other_side = swap(side, 1)

    source_device = tile_in // blocks_dev
    group = source_device // col_count
    local = tile_in % blocks_dev
    plane_gap = (group // PLANE - row_pos // PLANE) % planes
    other_chip = ((group // 2) ^ (row_pos // 2)) & 1
    other_core = (group ^ row_pos) & 1
    core = row_pos & 1
    below = plane_gap > planes // 2
    steps = jnp.where(below, planes - plane_gap, plane_gap)
    holder = jnp.where(below, 0, 1)
    from_core = group & 1
    sent_by_other = from_core ^ holder
    in_half = jnp.where(
        other_chip == 0,
        (steps - 1) * 2 + sent_by_other,
        4 + jnp.where(plane_gap == 0, 0, 1 + (steps - 1) * 2 + sent_by_other),
    )
    half_slots = 9
    holder = jnp.where(plane_gap == 0, from_core, holder)
    slot = 2 + in_half + jnp.where(holder == core, 0, half_slots)
    slot = jnp.where((plane_gap == 0) & (other_chip == 0), other_core, slot)
    src_index = slot * blocks_dev + local
    dst_index = tile_out - row_pos * col_count * blocks_dev

    tiles = tile_values.shape[0]
    sends = pl.pallas_call(
        tile_kernel,
        out_shape=jax.ShapeDtypeStruct((col_count, nodes, feat), BF),
        in_specs=[smem(), smem()] + [vmem()] * 8,
        out_specs=vmem(),
        scratch_shapes=[
            pltpu.VMEM((20 * nodes, feat), BF),
            pltpu.VMEM((col_count * blocks_dev, SIDE, feat), F32),
        ],
        compiler_params=params,
        cost_estimate=pl.CostEstimate(
            flops=2 * tiles * SIDE * SIDE * feat, bytes_accessed=6 << 20, transcendentals=0
        ),
        name="tiles",
    )(src_index, dst_index, tile_values, adjoint, beside, near, far, side, other_near, other_side)

    sends, wsum = lax.optimization_barrier((sends, wsum))
    got = lax.all_to_all(sends, "col", 0, 0)
    for bit in col_bits[2:]:
        wsum = with_partner(wsum, "col", bit)
    for bit in row_bits:
        wsum = with_partner(wsum, "row", bit)
    scale = 1.0 / float(nodes * row_count * col_count) ** 0.5
    node_grad, weight_grad = pl.pallas_call(
        functools.partial(finish_kernel, scale),
        out_shape=(jax.ShapeDtypeStruct((nodes, feat), BF), jax.ShapeDtypeStruct((feat, feat), F32)),
        in_specs=[vmem(), vmem()],
        out_specs=(vmem(), vmem()),
        compiler_params=params,
        name="finish",
    )(got, wsum)
    return (node_grad, weight_grad)


def solution(mesh):
    split = P(("row", "col"))
    return jax.shard_map(
        on_device,
        mesh=mesh,
        in_specs=(split, split, split, P(), split, split, split, split),
        out_specs=(split, P()),
        check_vma=False,
    )
```

```python
import functools

import jax
import jax.numpy as jnp
from jax import lax
from jax.experimental import pallas as pl
from jax.experimental.pallas import tpu as pltpu
from jax.sharding import PartitionSpec as P

BF = jnp.bfloat16
F32 = jnp.float32
SIDE = 128
PLANE = 4


def dot(a, b, contract):
    return lax.dot_general(a, b, ((contract[:1], contract[1:]), ((), ())), preferred_element_type=F32)


def adjoint_kernel(order_in, cot_in, pre_in, agg_in, w_in, out_ref, order_ref, cot_ref, pre_ref, agg_ref, w_ref, sems):
    ins = (order_in, cot_in, pre_in, w_in, agg_in)
    held = (order_ref, cot_ref, pre_ref, w_ref, agg_ref)
    copies = [pltpu.make_async_copy(a, b, sems.at[i]) for i, (a, b) in enumerate(zip(ins, held))]
    for copy in copies:
        copy.start()
    for copy in copies:
        copy.wait()
    rows = cot_ref.shape[0]
    cot = cot_ref[...]
    row_id = lax.broadcasted_iota(jnp.int32, (rows, SIDE), 0)
    base = (lax.axis_index("row") * lax.axis_size("col") + lax.axis_index("col")) * rows
    total = jnp.zeros(w_ref.shape, F32)
    for b in range(rows // SIDE):
        span = slice(b * SIDE, (b + 1) * SIDE)
        local = order_ref[b : b + 1, :] - base
        pick = jnp.where(row_id == local, 1.0, 0.0).astype(BF)
        grad_rows = dot(pick, cot, (0, 0))
        grad_pre = jnp.where(pre_ref[span, :].astype(F32) > 0, grad_rows, 0.0).astype(BF)
        total += dot(agg_ref[span, :], grad_pre, (0, 0))
        out_ref[span, :] = dot(grad_pre, w_ref[...], (1, 1)).astype(BF)
    high = total.astype(BF)
    out_ref[rows : rows + total.shape[0], :] = high
    out_ref[rows + total.shape[0] :, :] = (total - high.astype(F32)).astype(BF)


def whole(pair):
    feat = pair.shape[0] // 2
    return pair[:feat].astype(F32) + pair[feat:].astype(F32)


def chip_kernel(own, beside, out_ref, weight_ref):
    nodes = out_ref.shape[0] // 2 - SIDE // 2
    out_ref[:nodes, :] = own[:nodes, :]
    out_ref[nodes : 2 * nodes, :] = beside[:nodes, :]
    weight = (whole(own[nodes:, :]) + whole(beside[nodes:, :])).astype(BF)
    out_ref[2 * nodes :, :] = weight
    weight_ref[...] = weight


def across_kernel(beside, near, far, third, fourth, out_ref, weights_ref):
    nodes = out_ref.shape[0] // 5
    out_ref[:nodes, :] = beside[:nodes, :]
    out_ref[nodes : 3 * nodes, :] = near[: 2 * nodes, :]
    out_ref[3 * nodes :, :] = far[: 2 * nodes, :]
    feat = third.shape[0]
    weights_ref[:feat, :] = near[2 * nodes :, :]
    weights_ref[feat : 2 * feat, :] = far[2 * nodes :, :]
    weights_ref[2 * feat : 3 * feat, :] = third[...]
    weights_ref[3 * feat :, :] = fourth[...]


def plane_kernel(weight, weights, other, out_ref, held):
    planes = held.shape[0]
    row = lax.axis_index("row")
    at, way = lax.div(row, PLANE), 2 * lax.rem(row, 2) - 1
    feat = weight.shape[0]

    def put(steps, value):
        held[lax.rem(at + steps + planes, planes)] = value

    put(0, weight[...])
    put(4, weights[3 * feat :, :])
    for steps in (1, 2, 3):
        span = slice((steps - 1) * feat, steps * feat)
        put(steps * way, weights[span, :])
        put(-steps * way, other[span, :])
    total = held[0].astype(F32)
    for p in range(1, planes):
        total += held[p].astype(F32)
    out_ref[...] = total


def block_place(block, row, planes, cols, blocks):
    device = lax.div(block, blocks)
    group = lax.div(device, cols)
    gap = lax.rem(lax.div(group, PLANE) - lax.div(row, PLANE) + planes, planes)
    core = lax.rem(group, 2)
    same_core = core == lax.rem(row, 2)
    same_chip = lax.rem(lax.div(group, 2), 2) == lax.rem(lax.div(row, 2), 2)
    below = gap > planes // 2
    steps = jnp.where(below, planes - gap, gap)
    receiver = jnp.where(gap == 0, 1 - core, jnp.where(below, 0, 1))
    place = (steps - 1) * 2 + jnp.where(core == receiver, 0, 1)
    place = jnp.where(same_chip, place, jnp.where(gap == 0, 4, 5 + place))
    slot = 2 + place + jnp.where(receiver == lax.rem(row, 2), 0, 9)
    slot = jnp.where((gap == 0) & same_chip, jnp.where(same_core, 0, 1), slot)
    return slot * blocks + lax.rem(block, blocks)


def tile_kernel(
    in_ref, to_ref, tiles_ref, own, beside, near, far, side, other, other_side, wsum, wacross,
    direct_ref, keep_ref, give_ref, blocks_ref, acc_ref,
):
    cols = direct_ref.shape[0]
    half = cols // 2
    share = direct_ref.shape[1] - SIDE
    blocks = acc_ref.shape[0] // cols
    nodes = blocks * SIDE
    rows = near.shape[0]
    at = 0
    for piece in (
        own[:nodes, :],
        beside[:nodes, :],
        near[: 2 * nodes, :],
        far[: 2 * nodes, :],
        side[...],
        other[: 2 * nodes, :],
        other[rows : rows + 2 * nodes, :],
        other_side[...],
    ):
        blocks_ref[at : at + piece.shape[0], :] = piece
        at += piece.shape[0]
    acc_ref[...] = jnp.zeros_like(acc_ref)
    row, col = lax.axis_index("row"), lax.axis_index("col")
    planes = lax.axis_size("row") // PLANE

    def one(t, carry):
        at = pl.multiple_of(block_place(in_ref[t], row, planes, cols, blocks) * SIDE, SIDE)
        to = to_ref[t] - row * cols * blocks
        acc_ref[to] += dot(tiles_ref[t], blocks_ref[pl.ds(at, SIDE), :], (1, 0))
        return carry

    lax.fori_loop(0, tiles_ref.shape[0], one, 0, unroll=8)
    weight = (wsum[...] + wacross[...]).astype(BF)
    for c in range(cols):
        direct_ref[c, :SIDE, :] = acc_ref[c * blocks].astype(BF)
        z = c % half
        direct_ref[c, SIDE:, :] = weight[z * share : (z + 1) * share, :]
    mine = lax.div(col, half) * half
    theirs = half - mine
    for z in range(half):
        for b in range(1, blocks):
            span = slice((b - 1) * SIDE, b * SIDE)
            keep_ref[z, span, :] = acc_ref[(mine + z) * blocks + b]
            give_ref[z, span, :] = acc_ref[(theirs + z) * blocks + b].astype(BF)


def first_kernel(direct_ref, out_ref, weight_ref):
    share = direct_ref.shape[1] - SIDE
    total = direct_ref[0].astype(F32)
    for c in range(1, direct_ref.shape[0]):
        total += direct_ref[c].astype(F32)
    out_ref[...] = total[:SIDE].astype(BF)
    high = total[SIDE:].astype(BF)
    weight_ref[:share, :] = high
    weight_ref[share:, :] = (total[SIDE:] - high.astype(F32)).astype(BF)


def pair_kernel(keep_ref, got_ref, weight_ref, out_ref):
    rows = keep_ref.shape[1]
    for z in range(keep_ref.shape[0]):
        out_ref[z, :rows, :] = (keep_ref[z] + got_ref[z].astype(F32)).astype(BF)
        out_ref[z, rows:, :] = weight_ref[...]


def finish_kernel(scale, first_ref, got_ref, out_ref, wgrad_ref):
    half = got_ref.shape[0]
    rows = out_ref.shape[0] - SIDE
    share = wgrad_ref.shape[0] // half
    out_ref[:SIDE, :] = first_ref[...]
    total = got_ref[0, :rows, :].astype(F32)
    for z in range(1, half):
        total += got_ref[z, :rows, :].astype(F32)
    out_ref[SIDE:, :] = total.astype(BF)
    for z in range(half):
        wgrad_ref[z * share : (z + 1) * share, :] = whole(got_ref[z, rows:, :]) * scale


def vmem():
    return pl.BlockSpec(memory_space=pltpu.VMEM)


def smem():
    return pl.BlockSpec(memory_space=pltpu.SMEM)


def on_device(cotangent, pre_act, aggregated, weight, tile_values, tile_in, tile_out, order):
    row_count = lax.axis_size("row")
    col_count = lax.axis_size("col")
    nodes, feat = cotangent.shape
    blocks_dev = nodes // SIDE
    planes = row_count // PLANE
    params = pltpu.CompilerParams(vmem_limit_bytes=12 << 20)
    small = pltpu.CompilerParams(vmem_limit_bytes=4 << 20)

    adjoint = pl.pallas_call(
        adjoint_kernel,
        out_shape=jax.ShapeDtypeStruct((nodes + 2 * feat, feat), BF),
        in_specs=[pl.BlockSpec(memory_space=pltpu.HBM)] * 5,
        out_specs=vmem(),
        scratch_shapes=[
            pltpu.VMEM((blocks_dev, SIDE), jnp.int32),
            pltpu.VMEM((nodes, feat), BF),
            pltpu.VMEM((nodes, feat), BF),
            pltpu.VMEM((nodes, feat), BF),
            pltpu.VMEM((feat, feat), BF),
            pltpu.SemaphoreType.DMA((5,)),
        ],
        compiler_params=pltpu.CompilerParams(vmem_limit_bytes=60 << 20),
        name="adjoint",
    )(order.reshape(blocks_dev, SIDE), cotangent, pre_act, aggregated, weight)

    def swap(value, bit):
        return lax.ppermute(value, "row", [(i, i ^ bit) for i in range(row_count)])

    def to_plane(value, steps):
        pairs = [(i, (i + PLANE * (steps if i % 2 == 0 else -steps)) % row_count) for i in range(row_count)]
        return lax.ppermute(value, "row", pairs)

    beside = swap(adjoint, 1)
    chip, weight_sum = pl.pallas_call(
        chip_kernel,
        out_shape=(jax.ShapeDtypeStruct((2 * nodes + feat, feat), BF), jax.ShapeDtypeStruct((feat, feat), BF)),
        in_specs=[vmem()] * 2,
        out_specs=(vmem(), vmem()),
        compiler_params=small,
        name="chip",
    )(adjoint, beside)
    near = to_plane(chip, 1)
    far = to_plane(chip, 2)
    third = to_plane(weight_sum, 3)
    fourth = to_plane(weight_sum, 4)
    across, weight_sums = pl.pallas_call(
        across_kernel,
        out_shape=(jax.ShapeDtypeStruct((5 * nodes, feat), BF), jax.ShapeDtypeStruct((4 * feat, feat), BF)),
        in_specs=[vmem()] * 5,
        out_specs=(vmem(), vmem()),
        compiler_params=small,
        name="across",
    )(beside, near, far, third, fourth)
    side = swap(across, 2)
    other = swap(jnp.concatenate([near, far]), 1)
    other_weight = swap(weight_sums, 1)
    wsum = pl.pallas_call(
        plane_kernel,
        out_shape=jax.ShapeDtypeStruct((feat, feat), F32),
        in_specs=[vmem()] * 3,
        out_specs=vmem(),
        scratch_shapes=[pltpu.VMEM((planes, feat, feat), BF)],
        compiler_params=small,
        cost_estimate=pl.CostEstimate(flops=1000, bytes_accessed=1000, transcendentals=0),
        name="planes",
    )(weight_sum, weight_sums, other_weight)
    wacross = swap(wsum, 2)
    side, other, wacross = lax.optimization_barrier((side, other, wacross))
    other_side = swap(side, 1)

    tiles = tile_values.shape[0]
    half = col_count // 2
    share = feat // half
    rest = nodes - SIDE
    direct, keep, give = pl.pallas_call(
        tile_kernel,
        out_shape=(
            jax.ShapeDtypeStruct((col_count, SIDE + share, feat), BF),
            jax.ShapeDtypeStruct((half, rest, feat), F32),
            jax.ShapeDtypeStruct((half, rest, feat), BF),
        ),
        in_specs=[smem()] * 2 + [vmem()] * 10,
        out_specs=(vmem(),) * 3,
        scratch_shapes=[
            pltpu.VMEM((20 * nodes, feat), BF),
            pltpu.VMEM((col_count * blocks_dev, SIDE, feat), F32),
        ],
        compiler_params=params,
        cost_estimate=pl.CostEstimate(
            flops=2 * tiles * SIDE * SIDE * feat, bytes_accessed=6 << 20, transcendentals=0
        ),
        name="tiles",
    )(tile_in, tile_out, tile_values, adjoint, beside, near, far, side, other, other_side, wsum, wacross)

    got = lax.ppermute(give, "col", [(i, (i + half) % col_count) for i in range(col_count)])
    direct = lax.all_to_all(direct, "col", 0, 0)
    first, weight_share = pl.pallas_call(
        first_kernel,
        out_shape=(jax.ShapeDtypeStruct((SIDE, feat), BF), jax.ShapeDtypeStruct((2 * share, feat), BF)),
        in_specs=[vmem()],
        out_specs=(vmem(), vmem()),
        compiler_params=small,
        name="first",
    )(direct)
    pair = pl.pallas_call(
        pair_kernel,
        out_shape=jax.ShapeDtypeStruct((half, rest + 2 * share, feat), BF),
        in_specs=[vmem()] * 3,
        out_specs=vmem(),
        compiler_params=small,
        name="pair",
    )(keep, got, weight_share)
    groups = [list(range(half)), list(range(half, col_count))]
    summed = lax.all_to_all(pair, "col", 0, 0, axis_index_groups=groups)
    scale = 1.0 / float(nodes * row_count * col_count) ** 0.5
    node_grad, weight_grad = pl.pallas_call(
        functools.partial(finish_kernel, scale),
        out_shape=(jax.ShapeDtypeStruct((nodes, feat), BF), jax.ShapeDtypeStruct((feat, feat), F32)),
        in_specs=[vmem()] * 2,
        out_specs=(vmem(), vmem()),
        compiler_params=small,
        name="finish",
    )(first, summed)
    return (node_grad, weight_grad)


def solution(mesh):
    split = P(("row", "col"))
    return jax.shard_map(
        on_device,
        mesh=mesh,
        in_specs=(split, split, split, P(), split, split, split, split),
        out_specs=(split, P()),
        check_vma=False,
    )
```

```python
import functools

import jax
import jax.numpy as jnp
from jax import lax
from jax.experimental import pallas as pl
from jax.experimental.pallas import tpu as pltpu
from jax.sharding import PartitionSpec as P

BF = jnp.bfloat16
F32 = jnp.float32
SIDE = 128
PLANE = 4


def dot(a, b, contract):
    return lax.dot_general(a, b, ((contract[:1], contract[1:]), ((), ())), preferred_element_type=F32)


def adjoint_kernel(order_in, cot_in, pre_in, agg_in, w_in, out_ref, wpart_ref, order_ref, cot_ref, pre_ref, agg_ref, w_ref, sems):
    ins = (order_in, cot_in, pre_in, w_in, agg_in)
    held = (order_ref, cot_ref, pre_ref, w_ref, agg_ref)
    copies = [pltpu.make_async_copy(a, b, sems.at[i]) for i, (a, b) in enumerate(zip(ins, held))]
    for copy in copies:
        copy.start()
    for copy in copies:
        copy.wait()
    rows = cot_ref.shape[0]
    cot = cot_ref[...]
    row_id = lax.broadcasted_iota(jnp.int32, (rows, SIDE), 0)
    base = (lax.axis_index("row") * lax.axis_size("col") + lax.axis_index("col")) * rows
    total = jnp.zeros(wpart_ref.shape, F32)
    for b in range(rows // SIDE):
        span = slice(b * SIDE, (b + 1) * SIDE)
        local = order_ref[b : b + 1, :] - base
        pick = jnp.where(row_id == local, 1.0, 0.0).astype(BF)
        grad_rows = dot(pick, cot, (0, 0))
        grad_pre = jnp.where(pre_ref[span, :].astype(F32) > 0, grad_rows, 0.0).astype(BF)
        total += dot(agg_ref[span, :], grad_pre, (0, 0))
        out_ref[span, :] = dot(grad_pre, w_ref[...], (1, 1)).astype(BF)
    wpart_ref[...] = total


def block_place(block, row, planes, cols, blocks):
    device = lax.div(block, blocks)
    group = lax.div(device, cols)
    gap = lax.rem(lax.div(group, PLANE) - lax.div(row, PLANE) + planes, planes)
    core = lax.rem(group, 2)
    same_core = core == lax.rem(row, 2)
    same_chip = lax.rem(lax.div(group, 2), 2) == lax.rem(lax.div(row, 2), 2)
    below = gap > planes // 2
    steps = jnp.where(below, planes - gap, gap)
    receiver = jnp.where(gap == 0, 1 - core, jnp.where(below, 0, 1))
    place = (steps - 1) * 2 + jnp.where(core == receiver, 0, 1)
    place = jnp.where(same_chip, place, jnp.where(gap == 0, 4, 5 + place))
    slot = 2 + place + jnp.where(receiver == lax.rem(row, 2), 0, 9)
    slot = jnp.where((gap == 0) & same_chip, jnp.where(same_core, 0, 1), slot)
    return slot * blocks + lax.rem(block, blocks)


def tile_kernel(in_ref, to_ref, tiles_ref, own, beside, near, far, side, other_near, other_side, out_ref, blocks_ref, acc_ref):
    cols, rows, _ = out_ref.shape
    blocks = rows // SIDE
    at = 0
    for piece in (own, beside, near, far, side, other_near, other_side):
        blocks_ref[at : at + piece.shape[0], :] = piece[...]
        at += piece.shape[0]
    acc_ref[...] = jnp.zeros_like(acc_ref)
    row = lax.axis_index("row")
    planes = lax.axis_size("row") // PLANE

    def one(t, carry):
        at = pl.multiple_of(block_place(in_ref[t], row, planes, cols, blocks) * SIDE, SIDE)
        to = to_ref[t] - row * cols * blocks
        acc_ref[to] += dot(tiles_ref[t], blocks_ref[pl.ds(at, SIDE), :], (1, 0))
        return carry

    lax.fori_loop(0, tiles_ref.shape[0], one, 0, unroll=8)
    for c in range(cols):
        for b in range(blocks):
            out_ref[c, b * SIDE : (b + 1) * SIDE, :] = acc_ref[c * blocks + b].astype(BF)


def finish_kernel(scale, got_ref, wsum_ref, out_ref, wgrad_ref):
    total = got_ref[0].astype(F32)
    for c in range(1, got_ref.shape[0]):
        total += got_ref[c].astype(F32)
    out_ref[...] = total.astype(BF)
    wgrad_ref[...] = wsum_ref[...] * scale


def vmem():
    return pl.BlockSpec(memory_space=pltpu.VMEM)


def smem():
    return pl.BlockSpec(memory_space=pltpu.SMEM)


def on_device(cotangent, pre_act, aggregated, weight, tile_values, tile_in, tile_out, order):
    row_count = lax.axis_size("row")
    col_count = lax.axis_size("col")
    nodes, feat = cotangent.shape
    blocks_dev = nodes // SIDE
    params = pltpu.CompilerParams(vmem_limit_bytes=12 << 20)
    small = pltpu.CompilerParams(vmem_limit_bytes=4 << 20)

    adjoint, wpart = pl.pallas_call(
        adjoint_kernel,
        out_shape=(jax.ShapeDtypeStruct((nodes, feat), BF), jax.ShapeDtypeStruct((feat, feat), F32)),
        in_specs=[pl.BlockSpec(memory_space=pltpu.HBM)] * 5,
        out_specs=(vmem(), vmem()),
        scratch_shapes=[
            pltpu.VMEM((blocks_dev, SIDE), jnp.int32),
            pltpu.VMEM((nodes, feat), BF),
            pltpu.VMEM((nodes, feat), BF),
            pltpu.VMEM((nodes, feat), BF),
            pltpu.VMEM((feat, feat), BF),
            pltpu.SemaphoreType.DMA((5,)),
        ],
        compiler_params=pltpu.CompilerParams(vmem_limit_bytes=60 << 20),
        name="adjoint",
    )(order.reshape(blocks_dev, SIDE), cotangent, pre_act, aggregated, weight)

    def swap(value, bit):
        return lax.ppermute(value, "row", [(i, i ^ bit) for i in range(row_count)])

    def to_plane(value, steps):
        pairs = [(i, (i + PLANE * (steps if i % 2 == 0 else -steps)) % row_count) for i in range(row_count)]
        return lax.ppermute(value, "row", pairs)

    def partner(value, axis, bit):
        return lax.ppermute(value, axis, [(i, i ^ bit) for i in range(lax.axis_size(axis))])

    beside = swap(adjoint, 1)
    chip = jnp.concatenate([adjoint, beside])
    near = to_plane(chip, 1)
    far = to_plane(chip, 2)
    z_bits = [1 << k for k in reversed(range((col_count // 2 - 1).bit_length()))]
    late_bits = [("row", 1 << k) for k in range((row_count - 1).bit_length())] + [("col", col_count // 2)]
    wsum = wpart
    for bit in z_bits[:-2]:
        wsum = wsum + partner(wsum, "col", bit)
    across, wsum = lax.optimization_barrier((jnp.concatenate([beside, near, far]), wsum))
    side = swap(across, 2)
    other_near = swap(jnp.concatenate([near, far]), 1)
    for bit in z_bits[-2:-1]:
        wsum = wsum + partner(wsum, "col", bit)
    side, other_near, wsum = lax.optimization_barrier((side, other_near, wsum))
    wnext = [partner(wsum, "col", bit) for bit in z_bits[-1:]]
    other_side = swap(side, 1)

    tiles = tile_values.shape[0]
    sends = pl.pallas_call(
        tile_kernel,
        out_shape=jax.ShapeDtypeStruct((col_count, nodes, feat), BF),
        in_specs=[smem(), smem()] + [vmem()] * 8,
        out_specs=vmem(),
        scratch_shapes=[
            pltpu.VMEM((20 * nodes, feat), BF),
            pltpu.VMEM((col_count * blocks_dev, SIDE, feat), F32),
        ],
        compiler_params=params,
        cost_estimate=pl.CostEstimate(
            flops=2 * tiles * SIDE * SIDE * feat, bytes_accessed=6 << 20, transcendentals=0
        ),
        name="tiles",
    )(tile_in, tile_out, tile_values, adjoint, beside, near, far, side, other_near, other_side)

    sends, wsum, wnext = lax.optimization_barrier((sends, wsum, wnext))
    got = lax.all_to_all(sends, "col", 0, 0)
    for value in wnext:
        wsum = wsum + value
    for axis, bit in late_bits:
        wsum = wsum + partner(wsum, axis, bit)
    scale = 1.0 / float(nodes * row_count * col_count) ** 0.5
    node_grad, weight_grad = pl.pallas_call(
        functools.partial(finish_kernel, scale),
        out_shape=(jax.ShapeDtypeStruct((nodes, feat), BF), jax.ShapeDtypeStruct((feat, feat), F32)),
        in_specs=[vmem(), vmem()],
        out_specs=(vmem(), vmem()),
        compiler_params=small,
        name="finish",
    )(got, wsum)
    return (node_grad, weight_grad)


def solution(mesh):
    split = P(("row", "col"))
    return jax.shard_map(
        on_device,
        mesh=mesh,
        in_specs=(split, split, split, P(), split, split, split, split),
        out_specs=(split, P()),
        check_vma=False,
    )
```

```python
import functools

import jax
import jax.numpy as jnp
from jax import lax
from jax.experimental import pallas as pl
from jax.experimental.pallas import tpu as pltpu
from jax.sharding import PartitionSpec as P

BF = jnp.bfloat16
F32 = jnp.float32
SIDE = 128
PLANE = 4


def dot(a, b, contract):
    return lax.dot_general(a, b, ((contract[:1], contract[1:]), ((), ())), preferred_element_type=F32)


def adjoint_kernel(order_in, cot_in, pre_in, agg_in, w_in, out_ref, wpart_ref, order_ref, cot_ref, pre_ref, agg_ref, w_ref, sems):
    ins = (order_in, cot_in, pre_in, w_in, agg_in)
    held = (order_ref, cot_ref, pre_ref, w_ref, agg_ref)
    copies = [pltpu.make_async_copy(a, b, sems.at[i]) for i, (a, b) in enumerate(zip(ins, held))]
    for copy in copies:
        copy.start()
    for copy in copies:
        copy.wait()
    rows = cot_ref.shape[0]
    cot = cot_ref[...]
    row_id = lax.broadcasted_iota(jnp.int32, (rows, SIDE), 0)
    base = (lax.axis_index("row") * lax.axis_size("col") + lax.axis_index("col")) * rows
    total = jnp.zeros(w_ref.shape, F32)
    for b in range(rows // SIDE):
        span = slice(b * SIDE, (b + 1) * SIDE)
        local = order_ref[b : b + 1, :] - base
        pick = jnp.where(row_id == local, 1.0, 0.0).astype(BF)
        grad_rows = dot(pick, cot, (0, 0))
        grad_pre = jnp.where(pre_ref[span, :].astype(F32) > 0, grad_rows, 0.0).astype(BF)
        total += dot(agg_ref[span, :], grad_pre, (0, 0))
        out_ref[span, :] = dot(grad_pre, w_ref[...], (1, 1)).astype(BF)
    for z in range(wpart_ref.shape[0]):
        wpart_ref[z] = total.astype(BF)


def block_place(block, row, planes, cols, blocks):
    device = lax.div(block, blocks)
    group = lax.div(device, cols)
    gap = lax.rem(lax.div(group, PLANE) - lax.div(row, PLANE) + planes, planes)
    core = lax.rem(group, 2)
    same_core = core == lax.rem(row, 2)
    same_chip = lax.rem(lax.div(group, 2), 2) == lax.rem(lax.div(row, 2), 2)
    below = gap > planes // 2
    steps = jnp.where(below, planes - gap, gap)
    receiver = jnp.where(gap == 0, core, jnp.where(below, 0, 1))
    place = (steps - 1) * 2 + jnp.where(core == receiver, 0, 1)
    place = jnp.where(same_chip, place, jnp.where(gap == 0, 4, 5 + place))
    slot = 2 + place + jnp.where(receiver == lax.rem(row, 2), 0, 9)
    slot = jnp.where((gap == 0) & same_chip, jnp.where(same_core, 0, 1), slot)
    return slot * blocks + lax.rem(block, blocks)


def place_kernel(blocks, in_ref, out_ref, from_ref, to_ref):
    row, cols = lax.axis_index("row"), lax.axis_size("col")
    planes = lax.axis_size("row") // PLANE

    def one(t, carry):
        from_ref[t] = block_place(in_ref[t], row, planes, cols, blocks) * SIDE
        to_ref[t] = out_ref[t] - row * cols * blocks
        return carry

    lax.fori_loop(0, in_ref.shape[0], one, 0)


def tile_kernel(
    from_ref, to_ref, tiles_ref, own, beside, near, far, across, across_near, across_far, other,
    out_ref, blocks_ref, acc_ref, sent_ref, sems,
):
    cols, rows, _ = out_ref.shape
    blocks = rows // SIDE
    at = 0
    for piece in (own, beside, near, far, across, across_near, across_far, other):
        blocks_ref[at : at + piece.shape[0], :] = piece[...]
        at += piece.shape[0]
    acc_ref[...] = jnp.zeros_like(acc_ref)

    def one(t, carry):
        at = pl.multiple_of(from_ref[t], SIDE)
        acc_ref[to_ref[t]] += dot(tiles_ref[t], blocks_ref[pl.ds(at, SIDE), :], (1, 0))
        return carry

    lax.fori_loop(0, tiles_ref.shape[0], one, 0, unroll=8)
    copies = [pltpu.make_async_copy(sent_ref.at[c], out_ref.at[c], sems.at[c]) for c in range(cols)]
    for c in range(cols):
        for b in range(blocks):
            sent_ref[c, b * SIDE : (b + 1) * SIDE, :] = acc_ref[c * blocks + b].astype(BF)
        copies[c].start()
    for c in range(cols):
        copies[c].wait()


def finish_kernel(scale, got_ref, wsum_ref, out_ref, wgrad_ref):
    total = got_ref[0].astype(F32)
    for c in range(1, got_ref.shape[0]):
        total += got_ref[c].astype(F32)
    out_ref[...] = total.astype(BF)
    wgrad_ref[...] = wsum_ref[...] * scale


def vmem():
    return pl.BlockSpec(memory_space=pltpu.VMEM)


def smem():
    return pl.BlockSpec(memory_space=pltpu.SMEM)


def on_device(cotangent, pre_act, aggregated, weight, tile_values, tile_in, tile_out, order):
    row_count = lax.axis_size("row")
    col_count = lax.axis_size("col")
    nodes, feat = cotangent.shape
    blocks_dev = nodes // SIDE
    half = col_count // 2
    params = pltpu.CompilerParams(vmem_limit_bytes=12 << 20)
    small = pltpu.CompilerParams(vmem_limit_bytes=4 << 20)

    adjoint, wpart = pl.pallas_call(
        adjoint_kernel,
        out_shape=(jax.ShapeDtypeStruct((nodes, feat), BF), jax.ShapeDtypeStruct((half, feat, feat), BF)),
        in_specs=[pl.BlockSpec(memory_space=pltpu.HBM)] * 5,
        out_specs=(vmem(), vmem()),
        scratch_shapes=[
            pltpu.VMEM((blocks_dev, SIDE), jnp.int32),
            pltpu.VMEM((nodes, feat), BF),
            pltpu.VMEM((nodes, feat), BF),
            pltpu.VMEM((nodes, feat), BF),
            pltpu.VMEM((feat, feat), BF),
            pltpu.SemaphoreType.DMA((5,)),
        ],
        compiler_params=pltpu.CompilerParams(vmem_limit_bytes=60 << 20),
        name="adjoint",
    )(order.reshape(blocks_dev, SIDE), cotangent, pre_act, aggregated, weight)

    def swap(value, bit):
        return lax.ppermute(value, "row", [(i, i ^ bit) for i in range(row_count)])

    def to_plane(value, steps, chip_bit, wanted):
        pairs = [(i, ((i ^ chip_bit) + PLANE * (steps if i % 2 == 0 else -steps)) % row_count) for i in range(row_count)]
        return lax.ppermute(value, "row", [pair for pair in pairs if pair[0] % PLANE in wanted])

    beside = swap(adjoint, 1)
    across = swap(adjoint, 2)
    chip = jnp.concatenate([adjoint, beside])
    far = to_plane(chip, 2, 0, (0, 1, 2, 3))
    across_far = to_plane(chip, 2, 2, (1, 2))
    across_near = to_plane(chip, 1, 2, (0, 1, 2, 3))
    near = to_plane(chip, 1, 0, (0, 1, 2, 3))

    groups = [list(range(half)), list(range(half, col_count))]
    wz = lax.all_to_all(wpart, "col", 0, 0, axis_index_groups=groups)
    wsum = wz.astype(F32).sum(0)

    def partner(value, axis, bit):
        return lax.ppermute(value, axis, [(i, i ^ bit) for i in range(lax.axis_size(axis))])

    received = jnp.concatenate([near, far, across, across_near, across_far])
    received, wsum = lax.optimization_barrier((received, wsum))
    other = swap(received, 1)
    wnext = partner(wsum, "col", half)

    scalars = jax.ShapeDtypeStruct(tile_in.shape, jnp.int32)
    places, targets = pl.pallas_call(
        functools.partial(place_kernel, blocks_dev),
        out_shape=(scalars, scalars),
        in_specs=[smem()] * 2,
        out_specs=(smem(), smem()),
        compiler_params=small,
        name="places",
    )(tile_in, tile_out)
    tiles = tile_values.shape[0]
    sends = pl.pallas_call(
        tile_kernel,
        out_shape=jax.ShapeDtypeStruct((col_count, nodes, feat), BF),
        in_specs=[smem(), smem()] + [vmem()] * 9,
        out_specs=pl.BlockSpec(memory_space=pl.ANY),
        scratch_shapes=[
            pltpu.VMEM((20 * nodes, feat), BF),
            pltpu.VMEM((col_count * blocks_dev, SIDE, feat), F32),
            pltpu.VMEM((col_count, nodes, feat), BF),
            pltpu.SemaphoreType.DMA((col_count,)),
        ],
        compiler_params=params,
        cost_estimate=pl.CostEstimate(
            flops=2 * tiles * SIDE * SIDE * feat, bytes_accessed=6 << 20, transcendentals=0
        ),
        name="tiles",
    )(places, targets, tile_values, adjoint, beside, near, far, across, across_near, across_far, other)

    sends, wsum, wnext = lax.optimization_barrier((sends, wsum, wnext))
    got = lax.all_to_all(sends, "col", 0, 0)
    wsum = wsum + wnext
    for bit in [1 << k for k in range((row_count - 1).bit_length())]:
        wsum = wsum + partner(wsum, "row", bit)
    scale = 1.0 / float(nodes * row_count * col_count) ** 0.5
    node_grad, weight_grad = pl.pallas_call(
        functools.partial(finish_kernel, scale),
        out_shape=(jax.ShapeDtypeStruct((nodes, feat), BF), jax.ShapeDtypeStruct((feat, feat), F32)),
        in_specs=[vmem(), vmem()],
        out_specs=(vmem(), vmem()),
        compiler_params=small,
        name="finish",
    )(got, wsum)
    return (node_grad, weight_grad)


def solution(mesh):
    split = P(("row", "col"))
    return jax.shard_map(
        on_device,
        mesh=mesh,
        in_specs=(split, split, split, P(), split, split, split, split),
        out_specs=(split, P()),
        check_vma=False,
    )
```

```python
import functools

import jax
import jax.numpy as jnp
from jax import lax
from jax.experimental import pallas as pl
from jax.experimental.pallas import tpu as pltpu
from jax.sharding import PartitionSpec as P

BF = jnp.bfloat16
F32 = jnp.float32
SIDE = 128
PLANE = 4


def dot(a, b, contract):
    return lax.dot_general(a, b, ((contract[:1], contract[1:]), ((), ())), preferred_element_type=F32)


def block_place(block, row, planes, cols, blocks):
    device = lax.div(block, blocks)
    group = lax.div(device, cols)
    gap = lax.rem(lax.div(group, PLANE) - lax.div(row, PLANE) + planes, planes)
    core = lax.rem(group, 2)
    same_core = core == lax.rem(row, 2)
    same_chip = lax.rem(lax.div(group, 2), 2) == lax.rem(lax.div(row, 2), 2)
    below = gap > planes // 2
    steps = jnp.where(below, planes - gap, gap)
    receiver = jnp.where(gap == 0, core, jnp.where(below, 0, 1))
    first = jnp.where(steps == 2, jnp.where(same_chip, 7, 1), jnp.where(same_chip, 3, 5))
    place = jnp.where(gap == 0, 0, first + jnp.where(core == receiver, 0, 1))
    slot = 2 + place + jnp.where(receiver == lax.rem(row, 2), 0, 9)
    slot = jnp.where((gap == 0) & same_chip, jnp.where(same_core, 0, 1), slot)
    return slot * blocks + lax.rem(block, blocks)


def adjoint_kernel(
    order_in, cot_in, pre_in, agg_in, w_in, in_in, to_in, out_ref, wpart_ref, place_ref, target_ref,
    order_ref, cot_ref, pre_ref, agg_ref, w_ref, in_ref, to_ref, sems,
):
    ins = (order_in, cot_in, pre_in, w_in, agg_in, in_in, to_in)
    held = (order_ref, cot_ref, pre_ref, w_ref, agg_ref, in_ref, to_ref)
    copies = [pltpu.make_async_copy(a, b, sems.at[i]) for i, (a, b) in enumerate(zip(ins, held))]
    for copy in copies:
        copy.start()
    for copy in copies:
        copy.wait()
    rows = cot_ref.shape[0]
    row, cols, blocks = lax.axis_index("row"), lax.axis_size("col"), rows // SIDE
    place_ref[...] = block_place(in_ref[...], row, lax.axis_size("row") // PLANE, cols, blocks) * SIDE
    target_ref[...] = to_ref[...] - row * cols * blocks
    cot = cot_ref[...]
    row_id = lax.broadcasted_iota(jnp.int32, (rows, SIDE), 0)
    base = (lax.axis_index("row") * lax.axis_size("col") + lax.axis_index("col")) * rows
    total = jnp.zeros(w_ref.shape, F32)
    for b in range(rows // SIDE):
        span = slice(b * SIDE, (b + 1) * SIDE)
        local = order_ref[b : b + 1, :] - base
        pick = jnp.where(row_id == local, 1.0, 0.0).astype(BF)
        grad_rows = dot(pick, cot, (0, 0))
        grad_pre = jnp.where(pre_ref[span, :].astype(F32) > 0, grad_rows, 0.0).astype(BF)
        total += dot(agg_ref[span, :], grad_pre, (0, 0))
        out_ref[span, :] = dot(grad_pre, w_ref[...], (1, 1)).astype(BF)
    for z in range(wpart_ref.shape[0]):
        wpart_ref[z] = total.astype(BF)


def tile_kernel(
    from_ref, to_ref, tiles_ref, own, beside, received, other,
    out_ref, blocks_ref, acc_ref, sent_ref, sems,
):
    cols, rows, _ = out_ref.shape
    blocks = rows // SIDE
    at = 0
    for piece in (own, beside, received, other):
        blocks_ref[at : at + piece.shape[0], :] = piece[...]
        at += piece.shape[0]
    acc_ref[...] = jnp.zeros_like(acc_ref)

    def one(t, carry):
        at = pl.multiple_of(from_ref[0, t], SIDE)
        acc_ref[to_ref[0, t]] += dot(tiles_ref[t], blocks_ref[pl.ds(at, SIDE), :], (1, 0))
        return carry

    lax.fori_loop(0, tiles_ref.shape[0], one, 0, unroll=8)
    copies = [pltpu.make_async_copy(sent_ref.at[c], out_ref.at[c], sems.at[c]) for c in range(cols)]
    for c in range(cols):
        for b in range(blocks):
            sent_ref[c, b * SIDE : (b + 1) * SIDE, :] = acc_ref[c * blocks + b].astype(BF)
        copies[c].start()
    for c in range(cols):
        copies[c].wait()


def finish_kernel(scale, got_ref, wsum_ref, out_ref, wgrad_ref):
    total = got_ref[0].astype(F32)
    for c in range(1, got_ref.shape[0]):
        total += got_ref[c].astype(F32)
    out_ref[...] = total.astype(BF)
    wgrad_ref[...] = wsum_ref[...] * scale


def vmem():
    return pl.BlockSpec(memory_space=pltpu.VMEM)


def smem():
    return pl.BlockSpec(memory_space=pltpu.SMEM)


def on_device(cotangent, pre_act, aggregated, weight, tile_values, tile_in, tile_out, order):
    row_count = lax.axis_size("row")
    col_count = lax.axis_size("col")
    nodes, feat = cotangent.shape
    blocks_dev = nodes // SIDE
    half = col_count // 2
    params = pltpu.CompilerParams(vmem_limit_bytes=12 << 20)
    small = pltpu.CompilerParams(vmem_limit_bytes=4 << 20)

    tiles = tile_values.shape[0]
    scalars = jax.ShapeDtypeStruct((1, tiles), jnp.int32)
    adjoint, wpart, places, targets = pl.pallas_call(
        adjoint_kernel,
        out_shape=(jax.ShapeDtypeStruct((nodes, feat), BF), jax.ShapeDtypeStruct((half, feat, feat), BF), scalars, scalars),
        in_specs=[pl.BlockSpec(memory_space=pltpu.HBM)] * 7,
        out_specs=(vmem(),) * 4,
        scratch_shapes=[
            pltpu.VMEM((blocks_dev, SIDE), jnp.int32),
            pltpu.VMEM((nodes, feat), BF),
            pltpu.VMEM((nodes, feat), BF),
            pltpu.VMEM((nodes, feat), BF),
            pltpu.VMEM((feat, feat), BF),
            pltpu.VMEM((1, tiles), jnp.int32),
            pltpu.VMEM((1, tiles), jnp.int32),
            pltpu.SemaphoreType.DMA((7,)),
        ],
        compiler_params=pltpu.CompilerParams(vmem_limit_bytes=60 << 20),
        name="adjoint",
    )(order.reshape(blocks_dev, SIDE), cotangent, pre_act, aggregated, weight, tile_in.reshape(1, tiles), tile_out.reshape(1, tiles))

    def swap(value, bit):
        return lax.ppermute(value, "row", [(i, i ^ bit) for i in range(row_count)])

    def to_plane(value, steps, chip_bit, wanted):
        pairs = [(i, ((i ^ chip_bit) + PLANE * (steps if i % 2 == 0 else -steps)) % row_count) for i in range(row_count)]
        return lax.ppermute(value, "row", [pair for pair in pairs if pair[0] % PLANE in wanted])

    beside = swap(adjoint, 1)
    across = swap(adjoint, 2)
    chip = jnp.concatenate([adjoint, beside])
    far = to_plane(chip, 2, 0, (0, 1, 2, 3))
    across_far = to_plane(chip, 2, 2, (1, 2))
    across_near = to_plane(chip, 1, 2, (0, 1, 2, 3))
    near = to_plane(chip, 1, 0, (0, 1, 2, 3))

    groups = [list(range(half)), list(range(half, col_count))]
    wz = lax.all_to_all(wpart, "col", 0, 0, axis_index_groups=groups)
    wsum = wz.astype(F32).sum(0)

    def partner(value, axis, bit):
        return lax.ppermute(value, axis, [(i, i ^ bit) for i in range(lax.axis_size(axis))])

    received = jnp.concatenate([across, across_far, near, across_near, far])
    received, wsum = lax.optimization_barrier((received, wsum))
    other = swap(received, 1)
    sends = pl.pallas_call(
        tile_kernel,
        out_shape=jax.ShapeDtypeStruct((col_count, nodes, feat), BF),
        in_specs=[smem(), smem()] + [vmem()] * 5,
        out_specs=pl.BlockSpec(memory_space=pl.ANY),
        scratch_shapes=[
            pltpu.VMEM((20 * nodes, feat), BF),
            pltpu.VMEM((col_count * blocks_dev, SIDE, feat), F32),
            pltpu.VMEM((col_count, nodes, feat), BF),
            pltpu.SemaphoreType.DMA((col_count,)),
        ],
        compiler_params=params,
        cost_estimate=pl.CostEstimate(
            flops=2 * tiles * SIDE * SIDE * feat, bytes_accessed=6 << 20, transcendentals=0
        ),
        name="tiles",
    )(places, targets, tile_values, adjoint, beside, received, other)

    sends, wsum = lax.optimization_barrier((sends, wsum))
    got = lax.all_to_all(sends, "col", 0, 0)
    for bit in [1 << k for k in range((row_count - 1).bit_length())]:
        wsum = wsum + partner(wsum, "row", bit)
    wsum = wsum + partner(wsum, "col", half)
    scale = 1.0 / float(nodes * row_count * col_count) ** 0.5
    node_grad, weight_grad = pl.pallas_call(
        functools.partial(finish_kernel, scale),
        out_shape=(jax.ShapeDtypeStruct((nodes, feat), BF), jax.ShapeDtypeStruct((feat, feat), F32)),
        in_specs=[vmem(), vmem()],
        out_specs=(vmem(), vmem()),
        compiler_params=small,
        name="finish",
    )(got, wsum)
    return (node_grad, weight_grad)


def solution(mesh):
    split = P(("row", "col"))
    return jax.shard_map(
        on_device,
        mesh=mesh,
        in_specs=(split, split, split, P(), split, split, split, split),
        out_specs=(split, P()),
        check_vma=False,
    )
```

```python
import functools

import jax
import jax.numpy as jnp
from jax import lax
from jax.experimental import pallas as pl
from jax.experimental.pallas import tpu as pltpu
from jax.sharding import PartitionSpec as P

BF = jnp.bfloat16
F32 = jnp.float32
SIDE = 128
PLANE = 4


def dot(a, b, contract):
    return lax.dot_general(a, b, ((contract[:1], contract[1:]), ((), ())), preferred_element_type=F32)


def block_place(block, row, planes, cols, blocks):
    device = lax.div(block, blocks)
    group = lax.div(device, cols)
    gap = lax.rem(lax.div(group, PLANE) - lax.div(row, PLANE) + planes, planes)
    core = lax.rem(group, 2)
    same_core = core == lax.rem(row, 2)
    same_chip = lax.rem(lax.div(group, 2), 2) == lax.rem(lax.div(row, 2), 2)
    below = gap > planes // 2
    steps = jnp.where(below, planes - gap, gap)
    receiver = jnp.where(gap == 0, core, jnp.where(below, 0, 1))
    first = jnp.where(steps == 2, jnp.where(same_chip, 2, 0), jnp.where(same_chip, 5, 7))
    place = jnp.where(gap == 0, 4, first + jnp.where(core == receiver, 0, 1))
    slot = 2 + place + jnp.where(receiver == lax.rem(row, 2), 0, 9)
    slot = jnp.where((gap == 0) & same_chip, jnp.where(same_core, 0, 1), slot)
    return slot * blocks + lax.rem(block, blocks)


def adjoint_kernel(
    order_in, cot_in, pre_in, agg_in, w_in, in_in, to_in, out_ref, wpart_ref, place_ref, target_ref,
    order_ref, cot_ref, pre_ref, agg_ref, w_ref, in_ref, to_ref, sems,
):
    ins = (order_in, cot_in, pre_in, w_in, agg_in, in_in, to_in)
    held = (order_ref, cot_ref, pre_ref, w_ref, agg_ref, in_ref, to_ref)
    copies = [pltpu.make_async_copy(a, b, sems.at[i]) for i, (a, b) in enumerate(zip(ins, held))]
    for copy in copies:
        copy.start()
    for copy in copies:
        copy.wait()
    rows = cot_ref.shape[0]
    row, cols, blocks = lax.axis_index("row"), lax.axis_size("col"), rows // SIDE
    place_ref[...] = block_place(in_ref[...], row, lax.axis_size("row") // PLANE, cols, blocks) * SIDE
    target_ref[...] = to_ref[...] - row * cols * blocks
    cot = cot_ref[...]
    row_id = lax.broadcasted_iota(jnp.int32, (rows, SIDE), 0)
    base = (lax.axis_index("row") * lax.axis_size("col") + lax.axis_index("col")) * rows
    total = jnp.zeros(w_ref.shape, F32)
    for b in range(rows // SIDE):
        span = slice(b * SIDE, (b + 1) * SIDE)
        local = order_ref[b : b + 1, :] - base
        pick = jnp.where(row_id == local, 1.0, 0.0).astype(BF)
        grad_rows = dot(pick, cot, (0, 0))
        grad_pre = jnp.where(pre_ref[span, :].astype(F32) > 0, grad_rows, 0.0).astype(BF)
        total += dot(agg_ref[span, :], grad_pre, (0, 0))
        out_ref[span, :] = dot(grad_pre, w_ref[...], (1, 1)).astype(BF)
    for z in range(wpart_ref.shape[0]):
        wpart_ref[z] = total.astype(BF)


def tile_kernel(
    from_ref, to_ref, tiles_ref, own, beside, received, other,
    out_ref, blocks_ref, acc_ref, sent_ref, sems,
):
    cols, rows, _ = out_ref.shape
    blocks = rows // SIDE
    at = 0
    for piece in (own, beside, received, other):
        blocks_ref[at : at + piece.shape[0], :] = piece[...]
        at += piece.shape[0]
    acc_ref[...] = jnp.zeros_like(acc_ref)

    def one(t, carry):
        at = pl.multiple_of(from_ref[0, t], SIDE)
        acc_ref[to_ref[0, t]] += dot(tiles_ref[t], blocks_ref[pl.ds(at, SIDE), :], (1, 0))
        return carry

    lax.fori_loop(0, tiles_ref.shape[0], one, 0, unroll=8)
    copies = [pltpu.make_async_copy(sent_ref.at[c], out_ref.at[c], sems.at[c]) for c in range(cols)]
    for c in range(cols):
        for b in range(blocks):
            sent_ref[c, b * SIDE : (b + 1) * SIDE, :] = acc_ref[c * blocks + b].astype(BF)
        copies[c].start()
    for c in range(cols):
        copies[c].wait()


def finish_kernel(scale, got_ref, wsum_ref, out_ref, wgrad_ref):
    total = got_ref[0].astype(F32)
    for c in range(1, got_ref.shape[0]):
        total += got_ref[c].astype(F32)
    out_ref[...] = total.astype(BF)
    wgrad_ref[...] = wsum_ref[...] * scale


def vmem():
    return pl.BlockSpec(memory_space=pltpu.VMEM)


def smem():
    return pl.BlockSpec(memory_space=pltpu.SMEM)


def on_device(cotangent, pre_act, aggregated, weight, tile_values, tile_in, tile_out, order):
    row_count = lax.axis_size("row")
    col_count = lax.axis_size("col")
    nodes, feat = cotangent.shape
    blocks_dev = nodes // SIDE
    half = col_count // 2
    quad = half // 2
    params = pltpu.CompilerParams(vmem_limit_bytes=12 << 20)
    small = pltpu.CompilerParams(vmem_limit_bytes=4 << 20)

    tiles = tile_values.shape[0]
    scalars = jax.ShapeDtypeStruct((1, tiles), jnp.int32)
    adjoint, wpart, places, targets = pl.pallas_call(
        adjoint_kernel,
        out_shape=(jax.ShapeDtypeStruct((nodes, feat), BF), jax.ShapeDtypeStruct((quad, feat, feat), BF), scalars, scalars),
        in_specs=[pl.BlockSpec(memory_space=pltpu.HBM)] * 7,
        out_specs=(vmem(),) * 4,
        scratch_shapes=[
            pltpu.VMEM((blocks_dev, SIDE), jnp.int32),
            pltpu.VMEM((nodes, feat), BF),
            pltpu.VMEM((nodes, feat), BF),
            pltpu.VMEM((nodes, feat), BF),
            pltpu.VMEM((feat, feat), BF),
            pltpu.VMEM((1, tiles), jnp.int32),
            pltpu.VMEM((1, tiles), jnp.int32),
            pltpu.SemaphoreType.DMA((7,)),
        ],
        compiler_params=pltpu.CompilerParams(vmem_limit_bytes=60 << 20),
        name="adjoint",
    )(order.reshape(blocks_dev, SIDE), cotangent, pre_act, aggregated, weight, tile_in.reshape(1, tiles), tile_out.reshape(1, tiles))

    def swap(value, bit):
        return lax.ppermute(value, "row", [(i, i ^ bit) for i in range(row_count)])

    def to_plane(value, steps, chip_bit, wanted):
        pairs = [(i, ((i ^ chip_bit) + PLANE * (steps if i % 2 == 0 else -steps)) % row_count) for i in range(row_count)]
        return lax.ppermute(value, "row", [pair for pair in pairs if pair[0] % PLANE in wanted])

    beside = swap(adjoint, 1)
    across = swap(adjoint, 2)
    chip = jnp.concatenate([adjoint, beside])
    far = to_plane(chip, 2, 0, (0, 1, 2, 3))
    across_far = to_plane(chip, 2, 2, (1, 2))
    across_near = to_plane(chip, 1, 2, (0, 1, 2, 3))
    near = to_plane(chip, 1, 0, (0, 1, 2, 3))

    def partner(value, axis, bit):
        return lax.ppermute(value, axis, [(i, i ^ bit) for i in range(lax.axis_size(axis))])

    wpart, across = lax.optimization_barrier((wpart, across))
    groups = [list(range(i, i + quad)) for i in range(0, col_count, quad)]
    wsum = lax.all_to_all(wpart, "col", 0, 0, axis_index_groups=groups).astype(F32).sum(0)
    received = jnp.concatenate([across_far, far, across, near, across_near])
    received, wsum = lax.optimization_barrier((received, wsum))
    other = swap(received, 1)
    wnext = partner(wsum, "col", quad)
    sends = pl.pallas_call(
        tile_kernel,
        out_shape=jax.ShapeDtypeStruct((col_count, nodes, feat), BF),
        in_specs=[smem(), smem()] + [vmem()] * 5,
        out_specs=pl.BlockSpec(memory_space=pl.ANY),
        scratch_shapes=[
            pltpu.VMEM((20 * nodes, feat), BF),
            pltpu.VMEM((col_count * blocks_dev, SIDE, feat), F32),
            pltpu.VMEM((col_count, nodes, feat), BF),
            pltpu.SemaphoreType.DMA((col_count,)),
        ],
        compiler_params=params,
        cost_estimate=pl.CostEstimate(
            flops=2 * tiles * SIDE * SIDE * feat, bytes_accessed=6 << 20, transcendentals=0
        ),
        name="tiles",
    )(places, targets, tile_values, adjoint, beside, received, other)

    sends, wnext = lax.optimization_barrier((sends, wnext))
    got = lax.all_to_all(sends, "col", 0, 0)
    wsum = wsum + wnext
    for bit in (1, 2):
        wsum = wsum + partner(wsum, "row", bit)
    planes = (PLANE, 2 * PLANE, 3 * PLANE)
    one, two, three = [partner(wsum, "row", bits) for bits in planes]
    wsum = (wsum + one) + (two + three)
    wsum = wsum + partner(wsum, "row", 4 * PLANE)
    wsum = wsum + partner(wsum, "col", half)
    scale = 1.0 / float(nodes * row_count * col_count) ** 0.5
    node_grad, weight_grad = pl.pallas_call(
        functools.partial(finish_kernel, scale),
        out_shape=(jax.ShapeDtypeStruct((nodes, feat), BF), jax.ShapeDtypeStruct((feat, feat), F32)),
        in_specs=[vmem(), vmem()],
        out_specs=(vmem(), vmem()),
        compiler_params=small,
        name="finish",
    )(got, wsum)
    return (node_grad, weight_grad)


def solution(mesh):
    split = P(("row", "col"))
    return jax.shard_map(
        on_device,
        mesh=mesh,
        in_specs=(split, split, split, P(), split, split, split, split),
        out_specs=(split, P()),
        check_vma=False,
    )
```

```python
import functools

import jax
import jax.numpy as jnp
from jax import lax
from jax.experimental import pallas as pl
from jax.experimental.pallas import tpu as pltpu
from jax.sharding import PartitionSpec as P

BF = jnp.bfloat16
F32 = jnp.float32
SIDE = 128
PLANE = 4


def dot(a, b, contract):
    return lax.dot_general(a, b, ((contract[:1], contract[1:]), ((), ())), preferred_element_type=F32)


def block_place(block, row, planes, cols, blocks):
    device = lax.div(block, blocks)
    group = lax.div(device, cols)
    gap = lax.rem(lax.div(group, PLANE) - lax.div(row, PLANE) + planes, planes)
    core = lax.rem(group, 2)
    same_core = core == lax.rem(row, 2)
    same_chip = lax.rem(lax.div(group, 2), 2) == lax.rem(lax.div(row, 2), 2)
    below = gap > planes // 2
    steps = jnp.where(below, planes - gap, gap)
    receiver = jnp.where(gap == 0, core, jnp.where(below, 0, 1))
    first = jnp.where(steps == 2, jnp.where(same_chip, 7, 1), jnp.where(same_chip, 3, 5))
    place = jnp.where(gap == 0, 0, first + jnp.where(core == receiver, 0, 1))
    slot = 2 + place + jnp.where(receiver == lax.rem(row, 2), 0, 9)
    slot = jnp.where((gap == 0) & same_chip, jnp.where(same_core, 0, 1), slot)
    return slot * blocks + lax.rem(block, blocks)


def adjoint_kernel(
    order_in, cot_in, pre_in, agg_in, w_in, in_in, to_in, out_ref, wpart_ref, place_ref, target_ref,
    order_ref, cot_ref, pre_ref, agg_ref, w_ref, in_ref, to_ref, sems,
):
    ins = (order_in, cot_in, pre_in, w_in, agg_in, in_in, to_in)
    held = (order_ref, cot_ref, pre_ref, w_ref, agg_ref, in_ref, to_ref)
    copies = [pltpu.make_async_copy(a, b, sems.at[i]) for i, (a, b) in enumerate(zip(ins, held))]
    for copy in copies:
        copy.start()
    for copy in copies:
        copy.wait()
    rows = cot_ref.shape[0]
    row, cols, blocks = lax.axis_index("row"), lax.axis_size("col"), rows // SIDE
    place_ref[...] = block_place(in_ref[...], row, lax.axis_size("row") // PLANE, cols, blocks) * SIDE
    target_ref[...] = to_ref[...] - row * cols * blocks
    cot = cot_ref[...]
    row_id = lax.broadcasted_iota(jnp.int32, (rows, SIDE), 0)
    base = (lax.axis_index("row") * lax.axis_size("col") + lax.axis_index("col")) * rows
    total = jnp.zeros(w_ref.shape, F32)
    for b in range(rows // SIDE):
        span = slice(b * SIDE, (b + 1) * SIDE)
        local = order_ref[b : b + 1, :] - base
        pick = jnp.where(row_id == local, 1.0, 0.0).astype(BF)
        grad_rows = dot(pick, cot, (0, 0))
        grad_pre = jnp.where(pre_ref[span, :].astype(F32) > 0, grad_rows, 0.0).astype(BF)
        total += dot(agg_ref[span, :], grad_pre, (0, 0))
        out_ref[span, :] = dot(grad_pre, w_ref[...], (1, 1)).astype(BF)
    for z in range(wpart_ref.shape[0]):
        wpart_ref[z] = total.astype(BF)


def halves_kernel(parts_ref, out_ref):
    total = parts_ref[0].astype(F32)
    for z in range(1, parts_ref.shape[0]):
        total += parts_ref[z].astype(F32)
    high = total.astype(BF)
    out_ref[: total.shape[0], :] = high
    out_ref[total.shape[0] :, :] = (total - high.astype(F32)).astype(BF)


def tile_kernel(
    from_ref, to_ref, tiles_ref, own, beside, ours, theirs, out_ref, weight_ref, blocks_ref, acc_ref, sent_ref, sems
):
    cols, rows, _ = out_ref.shape
    blocks = rows // SIDE
    feat = weight_ref.shape[0]
    sets = ours.shape[0] - 2 * feat
    at = 0
    for piece in (own[...], beside[...], ours[:sets, :], theirs[:sets, :]):
        blocks_ref[at : at + piece.shape[0], :] = piece
        at += piece.shape[0]
    acc_ref[...] = jnp.zeros_like(acc_ref)

    def one(t, carry):
        at = pl.multiple_of(from_ref[0, t], SIDE)
        acc_ref[to_ref[0, t]] += dot(tiles_ref[t], blocks_ref[pl.ds(at, SIDE), :], (1, 0))
        return carry

    lax.fori_loop(0, tiles_ref.shape[0], one, 0, unroll=8)
    copies = [pltpu.make_async_copy(sent_ref.at[c], out_ref.at[c], sems.at[c]) for c in range(cols)]
    for c in range(cols):
        for b in range(blocks):
            sent_ref[c, b * SIDE : (b + 1) * SIDE, :] = acc_ref[c * blocks + b].astype(BF)
        copies[c].start()
    mine, yours = [
        pair[sets : sets + feat, :].astype(F32) + pair[sets + feat :, :].astype(F32) for pair in (ours, theirs)
    ]
    weight_ref[...] = mine + yours
    for c in range(cols):
        copies[c].wait()


def finish_kernel(scale, got_ref, wsum_ref, out_ref, wgrad_ref):
    total = got_ref[0].astype(F32)
    for c in range(1, got_ref.shape[0]):
        total += got_ref[c].astype(F32)
    out_ref[...] = total.astype(BF)
    wgrad_ref[...] = wsum_ref[...] * scale


def vmem():
    return pl.BlockSpec(memory_space=pltpu.VMEM)


def smem():
    return pl.BlockSpec(memory_space=pltpu.SMEM)


def on_device(cotangent, pre_act, aggregated, weight, tile_values, tile_in, tile_out, order):
    row_count = lax.axis_size("row")
    col_count = lax.axis_size("col")
    nodes, feat = cotangent.shape
    blocks_dev = nodes // SIDE
    half = col_count // 2
    params = pltpu.CompilerParams(vmem_limit_bytes=12 << 20)
    small = pltpu.CompilerParams(vmem_limit_bytes=4 << 20)

    tiles = tile_values.shape[0]
    scalars = jax.ShapeDtypeStruct((1, tiles), jnp.int32)
    adjoint, wpart, places, targets = pl.pallas_call(
        adjoint_kernel,
        out_shape=(jax.ShapeDtypeStruct((nodes, feat), BF), jax.ShapeDtypeStruct((half, feat, feat), BF), scalars, scalars),
        in_specs=[pl.BlockSpec(memory_space=pltpu.HBM)] * 7,
        out_specs=(vmem(),) * 4,
        scratch_shapes=[
            pltpu.VMEM((blocks_dev, SIDE), jnp.int32),
            pltpu.VMEM((nodes, feat), BF),
            pltpu.VMEM((nodes, feat), BF),
            pltpu.VMEM((nodes, feat), BF),
            pltpu.VMEM((feat, feat), BF),
            pltpu.VMEM((1, tiles), jnp.int32),
            pltpu.VMEM((1, tiles), jnp.int32),
            pltpu.SemaphoreType.DMA((7,)),
        ],
        compiler_params=pltpu.CompilerParams(vmem_limit_bytes=60 << 20),
        name="adjoint",
    )(order.reshape(blocks_dev, SIDE), cotangent, pre_act, aggregated, weight, tile_in.reshape(1, tiles), tile_out.reshape(1, tiles))

    def swap(value, bit):
        return lax.ppermute(value, "row", [(i, i ^ bit) for i in range(row_count)])

    def to_plane(value, steps, chip_bit, wanted):
        pairs = [(i, ((i ^ chip_bit) + PLANE * (steps if i % 2 == 0 else -steps)) % row_count) for i in range(row_count)]
        return lax.ppermute(value, "row", [pair for pair in pairs if pair[0] % PLANE in wanted])

    beside = swap(adjoint, 1)
    across = swap(adjoint, 2)
    chip = jnp.concatenate([adjoint, beside])
    far = to_plane(chip, 2, 0, (0, 1, 2, 3))
    across_far = to_plane(chip, 2, 2, (1, 2))
    across_near = to_plane(chip, 1, 2, (0, 1, 2, 3))
    near = to_plane(chip, 1, 0, (0, 1, 2, 3))

    groups = [list(range(half)), list(range(half, col_count))]
    wz = lax.all_to_all(wpart, "col", 0, 0, axis_index_groups=groups)
    halves = pl.pallas_call(
        halves_kernel,
        out_shape=jax.ShapeDtypeStruct((2 * feat, feat), BF),
        in_specs=[vmem()],
        out_specs=vmem(),
        compiler_params=small,
        name="halves",
    )(wz)

    def partner(value, axis, bit):
        return lax.ppermute(value, axis, [(i, i ^ bit) for i in range(lax.axis_size(axis))])

    received = jnp.concatenate([across, across_far, near, across_near, far, halves])
    other = swap(received, 1)

    sends, wsum = pl.pallas_call(
        tile_kernel,
        out_shape=(jax.ShapeDtypeStruct((col_count, nodes, feat), BF), jax.ShapeDtypeStruct((feat, feat), F32)),
        in_specs=[smem(), smem()] + [vmem()] * 5,
        out_specs=(pl.BlockSpec(memory_space=pl.ANY), vmem()),
        scratch_shapes=[
            pltpu.VMEM((20 * nodes, feat), BF),
            pltpu.VMEM((col_count * blocks_dev, SIDE, feat), F32),
            pltpu.VMEM((col_count, nodes, feat), BF),
            pltpu.SemaphoreType.DMA((col_count,)),
        ],
        compiler_params=params,
        cost_estimate=pl.CostEstimate(
            flops=2 * tiles * SIDE * SIDE * feat, bytes_accessed=6 << 20, transcendentals=0
        ),
        name="tiles",
    )(places, targets, tile_values, adjoint, beside, received, other)

    got = lax.all_to_all(sends, "col", 0, 0)
    for bit in [1 << k for k in range(1, (row_count - 1).bit_length())]:
        wsum = wsum + partner(wsum, "row", bit)
    wsum = wsum + partner(wsum, "col", half)
    scale = 1.0 / float(nodes * row_count * col_count) ** 0.5
    node_grad, weight_grad = pl.pallas_call(
        functools.partial(finish_kernel, scale),
        out_shape=(jax.ShapeDtypeStruct((nodes, feat), BF), jax.ShapeDtypeStruct((feat, feat), F32)),
        in_specs=[vmem(), vmem()],
        out_specs=(vmem(), vmem()),
        compiler_params=small,
        name="finish",
    )(got, wsum)
    return (node_grad, weight_grad)


def solution(mesh):
    split = P(("row", "col"))
    return jax.shard_map(
        on_device,
        mesh=mesh,
        in_specs=(split, split, split, P(), split, split, split, split),
        out_specs=(split, P()),
        check_vma=False,
    )
```

```python
import functools

import jax
import jax.numpy as jnp
from jax import lax
from jax.experimental import pallas as pl
from jax.experimental.pallas import tpu as pltpu
from jax.sharding import PartitionSpec as P

BF = jnp.bfloat16
F32 = jnp.float32
SIDE = 128
PLANE = 4


def dot(a, b, contract):
    return lax.dot_general(a, b, ((contract[:1], contract[1:]), ((), ())), preferred_element_type=F32)


def block_place(block, row, planes, cols, blocks):
    device = lax.div(block, blocks)
    group = lax.div(device, cols)
    gap = lax.rem(lax.div(group, PLANE) - lax.div(row, PLANE) + planes, planes)
    core = lax.rem(group, 2)
    same_core = core == lax.rem(row, 2)
    same_chip = lax.rem(lax.div(group, 2), 2) == lax.rem(lax.div(row, 2), 2)
    below = gap > planes // 2
    steps = jnp.where(below, planes - gap, gap)
    receiver = jnp.where(gap == 0, core, jnp.where(below, 0, 1))
    first = jnp.where(steps == 2, jnp.where(same_chip, 7, 1), jnp.where(same_chip, 3, 5))
    place = jnp.where(gap == 0, 0, first + jnp.where(core == receiver, 0, 1))
    slot = 2 + place + jnp.where(receiver == lax.rem(row, 2), 0, 9)
    slot = jnp.where((gap == 0) & same_chip, jnp.where(same_core, 0, 1), slot)
    return slot * blocks + lax.rem(block, blocks)


def adjoint_kernel(
    order_in, cot_in, pre_in, agg_in, w_in, in_in, to_in, out_ref, wpart_ref, place_ref, target_ref,
    order_ref, cot_ref, pre_ref, agg_ref, w_ref, in_ref, to_ref, sems,
):
    ins = (order_in, cot_in, pre_in, w_in, agg_in, in_in, to_in)
    held = (order_ref, cot_ref, pre_ref, w_ref, agg_ref, in_ref, to_ref)
    copies = [pltpu.make_async_copy(a, b, sems.at[i]) for i, (a, b) in enumerate(zip(ins, held))]
    for copy in copies:
        copy.start()
    for copy in copies:
        copy.wait()
    rows = cot_ref.shape[0]
    row, cols, blocks = lax.axis_index("row"), lax.axis_size("col"), rows // SIDE
    place_ref[...] = block_place(in_ref[...], row, lax.axis_size("row") // PLANE, cols, blocks) * SIDE
    target_ref[...] = to_ref[...] - row * cols * blocks
    cot = cot_ref[...]
    row_id = lax.broadcasted_iota(jnp.int32, (rows, SIDE), 0)
    base = (lax.axis_index("row") * lax.axis_size("col") + lax.axis_index("col")) * rows
    total = jnp.zeros(w_ref.shape, F32)
    for b in range(rows // SIDE):
        span = slice(b * SIDE, (b + 1) * SIDE)
        local = order_ref[b : b + 1, :] - base
        pick = jnp.where(row_id == local, 1.0, 0.0).astype(BF)
        grad_rows = dot(pick, cot, (0, 0))
        grad_pre = jnp.where(pre_ref[span, :].astype(F32) > 0, grad_rows, 0.0).astype(BF)
        total += dot(agg_ref[span, :], grad_pre, (0, 0))
        out_ref[span, :] = dot(grad_pre, w_ref[...], (1, 1)).astype(BF)
    for z in range(wpart_ref.shape[0]):
        wpart_ref[z] = total.astype(BF)


def halves_kernel(parts_ref, out_ref):
    total = parts_ref[0].astype(F32)
    for z in range(1, parts_ref.shape[0]):
        total += parts_ref[z].astype(F32)
    high = total.astype(BF)
    out_ref[: total.shape[0], :] = high
    out_ref[total.shape[0] :, :] = (total - high.astype(F32)).astype(BF)


def tile_kernel(
    from_ref, to_ref, tiles_ref, own, beside, ours, theirs, out_ref, weight_ref, blocks_ref, acc_ref, sent_ref, sems
):
    cols, rows, _ = out_ref.shape
    blocks = rows // SIDE
    feat = weight_ref.shape[0]
    sets = ours.shape[0] - 2 * feat
    at = 0
    for piece in (own[...], beside[...], ours[:sets, :], theirs[:sets, :]):
        blocks_ref[at : at + piece.shape[0], :] = piece
        at += piece.shape[0]
    acc_ref[...] = jnp.zeros_like(acc_ref)

    def one(t, carry):
        at = pl.multiple_of(from_ref[0, t], SIDE)
        acc_ref[to_ref[0, t]] += dot(tiles_ref[t], blocks_ref[pl.ds(at, SIDE), :], (1, 0))
        return carry

    lax.fori_loop(0, tiles_ref.shape[0], one, 0, unroll=8)
    copies = [pltpu.make_async_copy(sent_ref.at[c], out_ref.at[c], sems.at[c]) for c in range(cols)]
    for c in range(cols):
        for b in range(blocks):
            sent_ref[c, b * SIDE : (b + 1) * SIDE, :] = acc_ref[c * blocks + b].astype(BF)
        copies[c].start()
    mine, yours = [
        pair[sets : sets + feat, :].astype(F32) + pair[sets + feat :, :].astype(F32) for pair in (ours, theirs)
    ]
    weight_ref[...] = mine + yours
    for c in range(cols):
        copies[c].wait()


def finish_kernel(scale, got_ref, wsum_ref, out_ref, wgrad_ref):
    total = got_ref[0].astype(F32)
    for c in range(1, got_ref.shape[0]):
        total += got_ref[c].astype(F32)
    out_ref[...] = total.astype(BF)
    wgrad_ref[...] = wsum_ref[...] * scale


def vmem():
    return pl.BlockSpec(memory_space=pltpu.VMEM)


def smem():
    return pl.BlockSpec(memory_space=pltpu.SMEM)


def on_device(cotangent, pre_act, aggregated, weight, tile_values, tile_in, tile_out, order):
    row_count = lax.axis_size("row")
    col_count = lax.axis_size("col")
    nodes, feat = cotangent.shape
    blocks_dev = nodes // SIDE
    half = col_count // 2
    params = pltpu.CompilerParams(vmem_limit_bytes=12 << 20)
    small = pltpu.CompilerParams(vmem_limit_bytes=4 << 20)

    tiles = tile_values.shape[0]
    scalars = jax.ShapeDtypeStruct((1, tiles), jnp.int32)
    adjoint, wpart, places, targets = pl.pallas_call(
        adjoint_kernel,
        out_shape=(jax.ShapeDtypeStruct((nodes, feat), BF), jax.ShapeDtypeStruct((half, feat, feat), BF), scalars, scalars),
        in_specs=[pl.BlockSpec(memory_space=pltpu.HBM)] * 7,
        out_specs=(vmem(),) * 4,
        scratch_shapes=[
            pltpu.VMEM((blocks_dev, SIDE), jnp.int32),
            pltpu.VMEM((nodes, feat), BF),
            pltpu.VMEM((nodes, feat), BF),
            pltpu.VMEM((nodes, feat), BF),
            pltpu.VMEM((feat, feat), BF),
            pltpu.VMEM((1, tiles), jnp.int32),
            pltpu.VMEM((1, tiles), jnp.int32),
            pltpu.SemaphoreType.DMA((7,)),
        ],
        compiler_params=pltpu.CompilerParams(vmem_limit_bytes=60 << 20),
        name="adjoint",
    )(order.reshape(blocks_dev, SIDE), cotangent, pre_act, aggregated, weight, tile_in.reshape(1, tiles), tile_out.reshape(1, tiles))

    def swap(value, bit):
        return lax.ppermute(value, "row", [(i, i ^ bit) for i in range(row_count)])

    def to_plane(value, steps, chip_bit, wanted):
        pairs = [(i, ((i ^ chip_bit) + PLANE * (steps if i % 2 == 0 else -steps)) % row_count) for i in range(row_count)]
        return lax.ppermute(value, "row", [pair for pair in pairs if pair[0] % PLANE in wanted])

    beside = swap(adjoint, 1)
    across = swap(adjoint, 2)
    chip = jnp.concatenate([adjoint, beside])
    far = to_plane(chip, 2, 0, (0, 1, 2, 3))
    across_far = to_plane(chip, 2, 2, (1, 2))
    across_near = to_plane(chip, 1, 2, (0, 1, 2, 3))
    near = to_plane(chip, 1, 0, (0, 1, 2, 3))

    groups = [list(range(half)), list(range(half, col_count))]
    wz = lax.all_to_all(wpart, "col", 0, 0, axis_index_groups=groups)
    halves = pl.pallas_call(
        halves_kernel,
        out_shape=jax.ShapeDtypeStruct((2 * feat, feat), BF),
        in_specs=[vmem()],
        out_specs=vmem(),
        compiler_params=small,
        name="halves",
    )(wz)

    def partner(value, axis, bit):
        return lax.ppermute(value, axis, [(i, i ^ bit) for i in range(lax.axis_size(axis))])

    received = jnp.concatenate([across, across_far, near, across_near, far, halves])
    other = swap(received, 1)

    sends, wsum = pl.pallas_call(
        tile_kernel,
        out_shape=(jax.ShapeDtypeStruct((col_count, nodes, feat), BF), jax.ShapeDtypeStruct((feat, feat), F32)),
        in_specs=[smem(), smem()] + [vmem()] * 5,
        out_specs=(pl.BlockSpec(memory_space=pl.ANY), vmem()),
        scratch_shapes=[
            pltpu.VMEM((20 * nodes, feat), BF),
            pltpu.VMEM((col_count * blocks_dev, SIDE, feat), F32),
            pltpu.VMEM((col_count, nodes, feat), BF),
            pltpu.SemaphoreType.DMA((col_count,)),
        ],
        compiler_params=params,
        cost_estimate=pl.CostEstimate(
            flops=2 * tiles * SIDE * SIDE * feat, bytes_accessed=6 << 20, transcendentals=0
        ),
        name="tiles",
    )(places, targets, tile_values, adjoint, beside, received, other)

    got = lax.all_to_all(sends, "col", 0, 0)
    for bit in [PLANE << k for k in range((row_count // PLANE - 1).bit_length())] + [2]:
        wsum = wsum + partner(wsum, "row", bit)
    wsum = wsum + partner(wsum, "col", half)
    scale = 1.0 / float(nodes * row_count * col_count) ** 0.5
    node_grad, weight_grad = pl.pallas_call(
        functools.partial(finish_kernel, scale),
        out_shape=(jax.ShapeDtypeStruct((nodes, feat), BF), jax.ShapeDtypeStruct((feat, feat), F32)),
        in_specs=[vmem(), vmem()],
        out_specs=(vmem(), vmem()),
        compiler_params=small,
        name="finish",
    )(got, wsum)
    return (node_grad, weight_grad)


def solution(mesh):
    split = P(("row", "col"))
    return jax.shard_map(
        on_device,
        mesh=mesh,
        in_specs=(split, split, split, P(), split, split, split, split),
        out_specs=(split, P()),
        check_vma=False,
    )
```

```python
import functools

import jax
import jax.numpy as jnp
from jax import lax
from jax.experimental import pallas as pl
from jax.experimental.pallas import tpu as pltpu
from jax.sharding import PartitionSpec as P

BF = jnp.bfloat16
F32 = jnp.float32
SIDE = 128
PLANE = 4


def dot(a, b, contract):
    return lax.dot_general(a, b, ((contract[:1], contract[1:]), ((), ())), preferred_element_type=F32)


def block_place(block, row, planes, cols, blocks):
    device = lax.div(block, blocks)
    group = lax.div(device, cols)
    gap = lax.rem(lax.div(group, PLANE) - lax.div(row, PLANE) + planes, planes)
    core = lax.rem(group, 2)
    same_core = core == lax.rem(row, 2)
    same_chip = lax.rem(lax.div(group, 2), 2) == lax.rem(lax.div(row, 2), 2)
    below = gap > planes // 2
    steps = jnp.where(below, planes - gap, gap)
    receiver = jnp.where(gap == 0, core, jnp.where(below, 0, 1))
    first = jnp.where(steps == 2, jnp.where(same_chip, 5, 1), jnp.where(same_chip, 3, 7))
    place = jnp.where(gap == 0, 0, first + jnp.where(core == receiver, 0, 1))
    slot = 2 + place + jnp.where(receiver == lax.rem(row, 2), 0, 9)
    slot = jnp.where((gap == 0) & same_chip, jnp.where(same_core, 0, 1), slot)
    return slot * blocks + lax.rem(block, blocks)


def adjoint_kernel(
    order_in, cot_in, pre_in, agg_in, w_in, in_in, to_in, out_ref, wpart_ref, place_ref, target_ref,
    order_ref, cot_ref, pre_ref, agg_ref, w_ref, in_ref, to_ref, sems,
):
    ins = (order_in, cot_in, pre_in, w_in, agg_in, in_in, to_in)
    held = (order_ref, cot_ref, pre_ref, w_ref, agg_ref, in_ref, to_ref)
    copies = [pltpu.make_async_copy(a, b, sems.at[i]) for i, (a, b) in enumerate(zip(ins, held))]
    for copy in copies:
        copy.start()
    for copy in copies:
        copy.wait()
    rows = cot_ref.shape[0]
    row, cols, blocks = lax.axis_index("row"), lax.axis_size("col"), rows // SIDE
    place_ref[...] = block_place(in_ref[...], row, lax.axis_size("row") // PLANE, cols, blocks) * SIDE
    target_ref[...] = to_ref[...] - row * cols * blocks
    cot = cot_ref[...]
    row_id = lax.broadcasted_iota(jnp.int32, (rows, SIDE), 0)
    base = (lax.axis_index("row") * lax.axis_size("col") + lax.axis_index("col")) * rows
    total = jnp.zeros(w_ref.shape, F32)
    for b in range(rows // SIDE):
        span = slice(b * SIDE, (b + 1) * SIDE)
        local = order_ref[b : b + 1, :] - base
        pick = jnp.where(row_id == local, 1.0, 0.0).astype(BF)
        grad_rows = dot(pick, cot, (0, 0))
        grad_pre = jnp.where(pre_ref[span, :].astype(F32) > 0, grad_rows, 0.0).astype(BF)
        total += dot(agg_ref[span, :], grad_pre, (0, 0))
        out_ref[span, :] = dot(grad_pre, w_ref[...], (1, 1)).astype(BF)
    for z in range(wpart_ref.shape[0]):
        wpart_ref[z] = total.astype(BF)


def halves_kernel(parts_ref, out_ref):
    total = parts_ref[0].astype(F32)
    for z in range(1, parts_ref.shape[0]):
        total += parts_ref[z].astype(F32)
    high = total.astype(BF)
    out_ref[: total.shape[0], :] = high
    out_ref[total.shape[0] :, :] = (total - high.astype(F32)).astype(BF)


def tile_kernel(
    from_ref, to_ref, tiles_ref, own, beside, ours, theirs, out_ref, weight_ref, blocks_ref, acc_ref, sent_ref, sems
):
    cols, rows, _ = out_ref.shape
    blocks = rows // SIDE
    feat = weight_ref.shape[0]
    sets = ours.shape[0] - 2 * feat
    at = 0
    for piece in (own[...], beside[...], ours[:sets, :], theirs[:sets, :]):
        blocks_ref[at : at + piece.shape[0], :] = piece
        at += piece.shape[0]
    acc_ref[...] = jnp.zeros_like(acc_ref)

    def one(t, carry):
        at = pl.multiple_of(from_ref[0, t], SIDE)
        acc_ref[to_ref[0, t]] += dot(tiles_ref[t], blocks_ref[pl.ds(at, SIDE), :], (1, 0))
        return carry

    lax.fori_loop(0, tiles_ref.shape[0], one, 0, unroll=8)
    copies = [pltpu.make_async_copy(sent_ref.at[c], out_ref.at[c], sems.at[c]) for c in range(cols)]
    for c in range(cols):
        for b in range(blocks):
            sent_ref[c, b * SIDE : (b + 1) * SIDE, :] = acc_ref[c * blocks + b].astype(BF)
        copies[c].start()
    mine, yours = [
        pair[sets : sets + feat, :].astype(F32) + pair[sets + feat :, :].astype(F32) for pair in (ours, theirs)
    ]
    weight_ref[...] = mine + yours
    for c in range(cols):
        copies[c].wait()


def finish_kernel(scale, got_ref, wsum_ref, out_ref, wgrad_ref):
    total = got_ref[0].astype(F32)
    for c in range(1, got_ref.shape[0]):
        total += got_ref[c].astype(F32)
    out_ref[...] = total.astype(BF)
    wgrad_ref[...] = wsum_ref[...] * scale


def vmem():
    return pl.BlockSpec(memory_space=pltpu.VMEM)


def smem():
    return pl.BlockSpec(memory_space=pltpu.SMEM)


def on_device(cotangent, pre_act, aggregated, weight, tile_values, tile_in, tile_out, order):
    row_count = lax.axis_size("row")
    col_count = lax.axis_size("col")
    nodes, feat = cotangent.shape
    blocks_dev = nodes // SIDE
    half = col_count // 2
    params = pltpu.CompilerParams(vmem_limit_bytes=12 << 20)
    small = pltpu.CompilerParams(vmem_limit_bytes=4 << 20)

    tiles = tile_values.shape[0]
    scalars = jax.ShapeDtypeStruct((1, tiles), jnp.int32)
    adjoint, wpart, places, targets = pl.pallas_call(
        adjoint_kernel,
        out_shape=(jax.ShapeDtypeStruct((nodes, feat), BF), jax.ShapeDtypeStruct((half, feat, feat), BF), scalars, scalars),
        in_specs=[pl.BlockSpec(memory_space=pltpu.HBM)] * 7,
        out_specs=(vmem(),) * 4,
        scratch_shapes=[
            pltpu.VMEM((blocks_dev, SIDE), jnp.int32),
            pltpu.VMEM((nodes, feat), BF),
            pltpu.VMEM((nodes, feat), BF),
            pltpu.VMEM((nodes, feat), BF),
            pltpu.VMEM((feat, feat), BF),
            pltpu.VMEM((1, tiles), jnp.int32),
            pltpu.VMEM((1, tiles), jnp.int32),
            pltpu.SemaphoreType.DMA((7,)),
        ],
        compiler_params=pltpu.CompilerParams(vmem_limit_bytes=60 << 20),
        name="adjoint",
    )(order.reshape(blocks_dev, SIDE), cotangent, pre_act, aggregated, weight, tile_in.reshape(1, tiles), tile_out.reshape(1, tiles))

    def swap(value, bit):
        return lax.ppermute(value, "row", [(i, i ^ bit) for i in range(row_count)])

    def to_plane(value, steps, chip_bit, wanted):
        pairs = [(i, ((i ^ chip_bit) + PLANE * (steps if i % 2 == 0 else -steps)) % row_count) for i in range(row_count)]
        return lax.ppermute(value, "row", [pair for pair in pairs if pair[0] % PLANE in wanted])

    beside = swap(adjoint, 1)
    across = swap(adjoint, 2)
    chip = jnp.concatenate([adjoint, beside])
    far = to_plane(chip, 2, 0, (0, 1, 2, 3))
    across_far = to_plane(chip, 2, 2, (1, 2))
    across_near = to_plane(chip, 1, 2, (0, 1, 2, 3))
    groups = [list(range(half)), list(range(half, col_count))]
    wz = lax.all_to_all(wpart, "col", 0, 0, axis_index_groups=groups)
    near_chip, wz = lax.optimization_barrier((chip, wz))
    near = to_plane(near_chip, 1, 0, (0, 1, 2, 3))

    halves = pl.pallas_call(
        halves_kernel,
        out_shape=jax.ShapeDtypeStruct((2 * feat, feat), BF),
        in_specs=[vmem()],
        out_specs=vmem(),
        compiler_params=small,
        name="halves",
    )(wz)

    def partner(value, axis, bit):
        return lax.ppermute(value, axis, [(i, i ^ bit) for i in range(lax.axis_size(axis))])

    received = jnp.concatenate([across, across_far, near, far, across_near, halves])
    other = swap(received, 1)

    sends, wsum = pl.pallas_call(
        tile_kernel,
        out_shape=(jax.ShapeDtypeStruct((col_count, nodes, feat), BF), jax.ShapeDtypeStruct((feat, feat), F32)),
        in_specs=[smem(), smem()] + [vmem()] * 5,
        out_specs=(pl.BlockSpec(memory_space=pl.ANY), vmem()),
        scratch_shapes=[
            pltpu.VMEM((20 * nodes, feat), BF),
            pltpu.VMEM((col_count * blocks_dev, SIDE, feat), F32),
            pltpu.VMEM((col_count, nodes, feat), BF),
            pltpu.SemaphoreType.DMA((col_count,)),
        ],
        compiler_params=params,
        cost_estimate=pl.CostEstimate(
            flops=2 * tiles * SIDE * SIDE * feat, bytes_accessed=6 << 20, transcendentals=0
        ),
        name="tiles",
    )(places, targets, tile_values, adjoint, beside, received, other)

    got = lax.all_to_all(sends, "col", 0, 0)
    for bit in [PLANE << k for k in range((row_count // PLANE - 1).bit_length())] + [2]:
        wsum = wsum + partner(wsum, "row", bit)
    wsum = wsum + partner(wsum, "col", half)
    scale = 1.0 / float(nodes * row_count * col_count) ** 0.5
    node_grad, weight_grad = pl.pallas_call(
        functools.partial(finish_kernel, scale),
        out_shape=(jax.ShapeDtypeStruct((nodes, feat), BF), jax.ShapeDtypeStruct((feat, feat), F32)),
        in_specs=[vmem(), vmem()],
        out_specs=(vmem(), vmem()),
        compiler_params=small,
        name="finish",
    )(got, wsum)
    return (node_grad, weight_grad)


def solution(mesh):
    split = P(("row", "col"))
    return jax.shard_map(
        on_device,
        mesh=mesh,
        in_specs=(split, split, split, P(), split, split, split, split),
        out_specs=(split, P()),
        check_vma=False,
    )
```

```python
import functools

import jax
import jax.numpy as jnp
from jax import lax
from jax.experimental import pallas as pl
from jax.experimental.pallas import tpu as pltpu
from jax.sharding import PartitionSpec as P

BF = jnp.bfloat16
F32 = jnp.float32
SIDE = 128
PLANE = 4


def dot(a, b, contract):
    return lax.dot_general(a, b, ((contract[:1], contract[1:]), ((), ())), preferred_element_type=F32)


def block_place(block, row, planes, cols, blocks):
    device = lax.div(block, blocks)
    group = lax.div(device, cols)
    gap = lax.rem(lax.div(group, PLANE) - lax.div(row, PLANE) + planes, planes)
    core = lax.rem(group, 2)
    same_core = core == lax.rem(row, 2)
    same_chip = lax.rem(lax.div(group, 2), 2) == lax.rem(lax.div(row, 2), 2)
    below = gap > planes // 2
    steps = jnp.where(below, planes - gap, gap)
    receiver = jnp.where(gap == 0, core, jnp.where(below, 0, 1))
    first = jnp.where(steps == 2, jnp.where(same_chip, 1, 7), jnp.where(same_chip, 3, 5))
    place = jnp.where(gap == 0, 0, first + jnp.where(core == receiver, 0, 1))
    slot = 2 + place + jnp.where(receiver == lax.rem(row, 2), 0, 9)
    slot = jnp.where((gap == 0) & same_chip, jnp.where(same_core, 0, 1), slot)
    return slot * blocks + lax.rem(block, blocks)


def adjoint_kernel(
    order_in, cot_in, pre_in, agg_in, w_in, in_in, to_in, out_ref, wpart_ref, place_ref, target_ref,
    order_ref, cot_ref, pre_ref, agg_ref, w_ref, in_ref, to_ref, sems,
):
    ins = (order_in, cot_in, pre_in, w_in, agg_in, in_in, to_in)
    held = (order_ref, cot_ref, pre_ref, w_ref, agg_ref, in_ref, to_ref)
    copies = [pltpu.make_async_copy(a, b, sems.at[i]) for i, (a, b) in enumerate(zip(ins, held))]
    for copy in copies:
        copy.start()
    for copy in copies:
        copy.wait()
    rows = cot_ref.shape[0]
    row, cols, blocks = lax.axis_index("row"), lax.axis_size("col"), rows // SIDE
    place_ref[...] = block_place(in_ref[...], row, lax.axis_size("row") // PLANE, cols, blocks) * SIDE
    target_ref[...] = to_ref[...] - row * cols * blocks
    cot = cot_ref[...]
    row_id = lax.broadcasted_iota(jnp.int32, (rows, SIDE), 0)
    base = (lax.axis_index("row") * lax.axis_size("col") + lax.axis_index("col")) * rows
    total = jnp.zeros(w_ref.shape, F32)
    for b in range(rows // SIDE):
        span = slice(b * SIDE, (b + 1) * SIDE)
        local = order_ref[b : b + 1, :] - base
        pick = jnp.where(row_id == local, 1.0, 0.0).astype(BF)
        grad_rows = dot(pick, cot, (0, 0))
        grad_pre = jnp.where(pre_ref[span, :].astype(F32) > 0, grad_rows, 0.0).astype(BF)
        total += dot(agg_ref[span, :], grad_pre, (0, 0))
        out_ref[span, :] = dot(grad_pre, w_ref[...], (1, 1)).astype(BF)
    for z in range(wpart_ref.shape[0]):
        wpart_ref[z] = total.astype(BF)


def halves_kernel(parts_ref, out_ref):
    total = parts_ref[0].astype(F32)
    for z in range(1, parts_ref.shape[0]):
        total += parts_ref[z].astype(F32)
    high = total.astype(BF)
    out_ref[: total.shape[0], :] = high
    out_ref[total.shape[0] :, :] = (total - high.astype(F32)).astype(BF)


def tile_kernel(
    from_ref, to_ref, tiles_ref, own, beside, ours, theirs, out_ref, weight_ref, blocks_ref, acc_ref, sent_ref, sems
):
    cols, rows, _ = out_ref.shape
    blocks = rows // SIDE
    feat = weight_ref.shape[0]
    sets = ours.shape[0] - 2 * feat
    at = 0
    for piece in (own[...], beside[...], ours[:sets, :], theirs[:sets, :]):
        blocks_ref[at : at + piece.shape[0], :] = piece
        at += piece.shape[0]
    acc_ref[...] = jnp.zeros_like(acc_ref)

    def one(t, carry):
        at = pl.multiple_of(from_ref[0, t], SIDE)
        acc_ref[to_ref[0, t]] += dot(tiles_ref[t], blocks_ref[pl.ds(at, SIDE), :], (1, 0))
        return carry

    lax.fori_loop(0, tiles_ref.shape[0], one, 0, unroll=8)
    copies = [pltpu.make_async_copy(sent_ref.at[c], out_ref.at[c], sems.at[c]) for c in range(cols)]
    for c in range(cols):
        for b in range(blocks):
            sent_ref[c, b * SIDE : (b + 1) * SIDE, :] = acc_ref[c * blocks + b].astype(BF)
        copies[c].start()
    mine, yours = [
        pair[sets : sets + feat, :].astype(F32) + pair[sets + feat :, :].astype(F32) for pair in (ours, theirs)
    ]
    weight_ref[...] = mine + yours
    for c in range(cols):
        copies[c].wait()


def finish_kernel(scale, got_ref, wsum_ref, out_ref, wgrad_ref):
    total = got_ref[0].astype(F32)
    for c in range(1, got_ref.shape[0]):
        total += got_ref[c].astype(F32)
    out_ref[...] = total.astype(BF)
    wgrad_ref[...] = wsum_ref[...] * scale


def vmem():
    return pl.BlockSpec(memory_space=pltpu.VMEM)


def smem():
    return pl.BlockSpec(memory_space=pltpu.SMEM)


def on_device(cotangent, pre_act, aggregated, weight, tile_values, tile_in, tile_out, order):
    row_count = lax.axis_size("row")
    col_count = lax.axis_size("col")
    nodes, feat = cotangent.shape
    blocks_dev = nodes // SIDE
    half = col_count // 2
    params = pltpu.CompilerParams(vmem_limit_bytes=12 << 20)
    small = pltpu.CompilerParams(vmem_limit_bytes=4 << 20)

    tiles = tile_values.shape[0]
    scalars = jax.ShapeDtypeStruct((1, tiles), jnp.int32)
    adjoint, wpart, places, targets = pl.pallas_call(
        adjoint_kernel,
        out_shape=(jax.ShapeDtypeStruct((nodes, feat), BF), jax.ShapeDtypeStruct((half, feat, feat), BF), scalars, scalars),
        in_specs=[pl.BlockSpec(memory_space=pltpu.HBM)] * 7,
        out_specs=(vmem(),) * 4,
        scratch_shapes=[
            pltpu.VMEM((blocks_dev, SIDE), jnp.int32),
            pltpu.VMEM((nodes, feat), BF),
            pltpu.VMEM((nodes, feat), BF),
            pltpu.VMEM((nodes, feat), BF),
            pltpu.VMEM((feat, feat), BF),
            pltpu.VMEM((1, tiles), jnp.int32),
            pltpu.VMEM((1, tiles), jnp.int32),
            pltpu.SemaphoreType.DMA((7,)),
        ],
        compiler_params=pltpu.CompilerParams(vmem_limit_bytes=60 << 20),
        name="adjoint",
    )(order.reshape(blocks_dev, SIDE), cotangent, pre_act, aggregated, weight, tile_in.reshape(1, tiles), tile_out.reshape(1, tiles))

    def swap(value, bit):
        return lax.ppermute(value, "row", [(i, i ^ bit) for i in range(row_count)])

    def to_plane(value, steps, chip_bit):
        pairs = [(i, ((i ^ chip_bit) + PLANE * (steps if i % 2 == 0 else -steps)) % row_count) for i in range(row_count)]
        return lax.ppermute(value, "row", pairs)

    beside = swap(adjoint, 1)
    across = swap(adjoint, 2)
    chip = jnp.concatenate([adjoint, beside])
    far = to_plane(chip, 2, 0)
    across_near = to_plane(chip, 1, 2)
    near = to_plane(chip, 1, 0)
    wanted = [(i, i ^ 2) for i in range(row_count) if i % PLANE in (1, 2)]
    across_far = lax.ppermute(far, "row", wanted)

    groups = [list(range(half)), list(range(half, col_count))]
    wz = lax.all_to_all(wpart, "col", 0, 0, axis_index_groups=groups)
    halves = pl.pallas_call(
        halves_kernel,
        out_shape=jax.ShapeDtypeStruct((2 * feat, feat), BF),
        in_specs=[vmem()],
        out_specs=vmem(),
        compiler_params=small,
        name="halves",
    )(wz)

    def partner(value, axis, bit):
        return lax.ppermute(value, axis, [(i, i ^ bit) for i in range(lax.axis_size(axis))])

    received = jnp.concatenate([across, far, near, across_near, across_far, halves])
    other = swap(received, 1)

    sends, wsum = pl.pallas_call(
        tile_kernel,
        out_shape=(jax.ShapeDtypeStruct((col_count, nodes, feat), BF), jax.ShapeDtypeStruct((feat, feat), F32)),
        in_specs=[smem(), smem()] + [vmem()] * 5,
        out_specs=(pl.BlockSpec(memory_space=pl.ANY), vmem()),
        scratch_shapes=[
            pltpu.VMEM((20 * nodes, feat), BF),
            pltpu.VMEM((col_count * blocks_dev, SIDE, feat), F32),
            pltpu.VMEM((col_count, nodes, feat), BF),
            pltpu.SemaphoreType.DMA((col_count,)),
        ],
        compiler_params=params,
        cost_estimate=pl.CostEstimate(
            flops=2 * tiles * SIDE * SIDE * feat, bytes_accessed=6 << 20, transcendentals=0
        ),
        name="tiles",
    )(places, targets, tile_values, adjoint, beside, received, other)

    got = lax.all_to_all(sends, "col", 0, 0)
    for bit in [PLANE << k for k in range((row_count // PLANE - 1).bit_length())] + [2]:
        wsum = wsum + partner(wsum, "row", bit)
    wsum = wsum + partner(wsum, "col", half)
    scale = 1.0 / float(nodes * row_count * col_count) ** 0.5
    node_grad, weight_grad = pl.pallas_call(
        functools.partial(finish_kernel, scale),
        out_shape=(jax.ShapeDtypeStruct((nodes, feat), BF), jax.ShapeDtypeStruct((feat, feat), F32)),
        in_specs=[vmem(), vmem()],
        out_specs=(vmem(), vmem()),
        compiler_params=small,
        name="finish",
    )(got, wsum)
    return (node_grad, weight_grad)


def solution(mesh):
    split = P(("row", "col"))
    return jax.shard_map(
        on_device,
        mesh=mesh,
        in_specs=(split, split, split, P(), split, split, split, split),
        out_specs=(split, P()),
        check_vma=False,
    )
```

```python
import functools

import jax
import jax.numpy as jnp
from jax import lax
from jax.experimental import pallas as pl
from jax.experimental.pallas import tpu as pltpu
from jax.sharding import PartitionSpec as P

BF = jnp.bfloat16
F32 = jnp.float32
SIDE = 128
PLANE = 4


def dot(a, b, contract):
    return lax.dot_general(a, b, ((contract[:1], contract[1:]), ((), ())), preferred_element_type=F32)


def block_place(block, row, planes, cols, blocks):
    device = lax.div(block, blocks)
    group = lax.div(device, cols)
    gap = lax.rem(lax.div(group, PLANE) - lax.div(row, PLANE) + planes, planes)
    core = lax.rem(group, 2)
    same_core = core == lax.rem(row, 2)
    same_chip = lax.rem(lax.div(group, 2), 2) == lax.rem(lax.div(row, 2), 2)
    below = gap > planes // 2
    steps = jnp.where(below, planes - gap, gap)
    receiver = jnp.where(gap == 0, core, jnp.where(below, 0, 1))
    first = jnp.where(steps == 2, jnp.where(same_chip, 0, 7), jnp.where(same_chip, 4, 2))
    place = jnp.where(gap == 0, 6, first + jnp.where(core == receiver, 0, 1))
    slot = 2 + place + jnp.where(receiver == lax.rem(row, 2), 0, 9)
    slot = jnp.where((gap == 0) & same_chip, jnp.where(same_core, 0, 1), slot)
    return slot * blocks + lax.rem(block, blocks)


def adjoint_kernel(
    order_in, cot_in, pre_in, agg_in, w_in, in_in, to_in, out_ref, wpart_ref, place_ref, target_ref,
    order_ref, cot_ref, pre_ref, agg_ref, w_ref, in_ref, to_ref, sems,
):
    ins = (order_in, cot_in, pre_in, w_in, agg_in, in_in, to_in)
    held = (order_ref, cot_ref, pre_ref, w_ref, agg_ref, in_ref, to_ref)
    copies = [pltpu.make_async_copy(a, b, sems.at[i]) for i, (a, b) in enumerate(zip(ins, held))]
    for copy in copies:
        copy.start()
    for copy in copies:
        copy.wait()
    rows = cot_ref.shape[0]
    row, cols, blocks = lax.axis_index("row"), lax.axis_size("col"), rows // SIDE
    place_ref[...] = block_place(in_ref[...], row, lax.axis_size("row") // PLANE, cols, blocks) * SIDE
    target_ref[...] = to_ref[...] - row * cols * blocks
    cot = cot_ref[...]
    row_id = lax.broadcasted_iota(jnp.int32, (rows, SIDE), 0)
    base = (lax.axis_index("row") * lax.axis_size("col") + lax.axis_index("col")) * rows
    total = jnp.zeros(w_ref.shape, F32)
    for b in range(rows // SIDE):
        span = slice(b * SIDE, (b + 1) * SIDE)
        local = order_ref[b : b + 1, :] - base
        pick = jnp.where(row_id == local, 1.0, 0.0).astype(BF)
        grad_rows = dot(pick, cot, (0, 0))
        grad_pre = jnp.where(pre_ref[span, :].astype(F32) > 0, grad_rows, 0.0).astype(BF)
        total += dot(agg_ref[span, :], grad_pre, (0, 0))
        out_ref[span, :] = dot(grad_pre, w_ref[...], (1, 1)).astype(BF)
    for z in range(wpart_ref.shape[0]):
        wpart_ref[z] = total.astype(BF)


def halves_kernel(parts_ref, out_ref):
    total = parts_ref[0].astype(F32)
    for z in range(1, parts_ref.shape[0]):
        total += parts_ref[z].astype(F32)
    high = total.astype(BF)
    out_ref[: total.shape[0], :] = high
    out_ref[total.shape[0] :, :] = (total - high.astype(F32)).astype(BF)


def tile_kernel(
    from_ref, to_ref, tiles_ref, own, beside, ours, theirs, out_ref, weight_ref, blocks_ref, acc_ref, sent_ref, sems
):
    cols, rows, _ = out_ref.shape
    blocks = rows // SIDE
    feat = weight_ref.shape[0]
    sets = ours.shape[0] - 2 * feat
    at = 0
    for piece in (own[...], beside[...], ours[:sets, :], theirs[:sets, :]):
        blocks_ref[at : at + piece.shape[0], :] = piece
        at += piece.shape[0]
    acc_ref[...] = jnp.zeros_like(acc_ref)

    def one(t, carry):
        at = pl.multiple_of(from_ref[0, t], SIDE)
        acc_ref[to_ref[0, t]] += dot(tiles_ref[t], blocks_ref[pl.ds(at, SIDE), :], (1, 0))
        return carry

    lax.fori_loop(0, tiles_ref.shape[0], one, 0, unroll=8)
    copies = [pltpu.make_async_copy(sent_ref.at[c], out_ref.at[c], sems.at[c]) for c in range(cols)]
    for c in range(cols):
        for b in range(blocks):
            sent_ref[c, b * SIDE : (b + 1) * SIDE, :] = acc_ref[c * blocks + b].astype(BF)
        copies[c].start()
    mine, yours = [
        pair[sets : sets + feat, :].astype(F32) + pair[sets + feat :, :].astype(F32) for pair in (ours, theirs)
    ]
    weight_ref[...] = mine + yours
    for c in range(cols):
        copies[c].wait()


def finish_kernel(scale, got_ref, wsum_ref, out_ref, wgrad_ref):
    total = got_ref[0].astype(F32)
    for c in range(1, got_ref.shape[0]):
        total += got_ref[c].astype(F32)
    out_ref[...] = total.astype(BF)
    wgrad_ref[...] = wsum_ref[...] * scale


def vmem():
    return pl.BlockSpec(memory_space=pltpu.VMEM)


def smem():
    return pl.BlockSpec(memory_space=pltpu.SMEM)


def on_device(cotangent, pre_act, aggregated, weight, tile_values, tile_in, tile_out, order):
    row_count = lax.axis_size("row")
    col_count = lax.axis_size("col")
    nodes, feat = cotangent.shape
    blocks_dev = nodes // SIDE
    half = col_count // 2
    params = pltpu.CompilerParams(vmem_limit_bytes=12 << 20)
    small = pltpu.CompilerParams(vmem_limit_bytes=4 << 20)

    tiles = tile_values.shape[0]
    scalars = jax.ShapeDtypeStruct((1, tiles), jnp.int32)
    adjoint, wpart, places, targets = pl.pallas_call(
        adjoint_kernel,
        out_shape=(jax.ShapeDtypeStruct((nodes, feat), BF), jax.ShapeDtypeStruct((half, feat, feat), BF), scalars, scalars),
        in_specs=[pl.BlockSpec(memory_space=pltpu.HBM)] * 7,
        out_specs=(vmem(),) * 4,
        scratch_shapes=[
            pltpu.VMEM((blocks_dev, SIDE), jnp.int32),
            pltpu.VMEM((nodes, feat), BF),
            pltpu.VMEM((nodes, feat), BF),
            pltpu.VMEM((nodes, feat), BF),
            pltpu.VMEM((feat, feat), BF),
            pltpu.VMEM((1, tiles), jnp.int32),
            pltpu.VMEM((1, tiles), jnp.int32),
            pltpu.SemaphoreType.DMA((7,)),
        ],
        compiler_params=pltpu.CompilerParams(vmem_limit_bytes=60 << 20),
        name="adjoint",
    )(order.reshape(blocks_dev, SIDE), cotangent, pre_act, aggregated, weight, tile_in.reshape(1, tiles), tile_out.reshape(1, tiles))

    def swap(value, bit):
        return lax.ppermute(value, "row", [(i, i ^ bit) for i in range(row_count)])

    def to_plane(value, steps, chip_bit):
        pairs = [(i, ((i ^ chip_bit) + PLANE * (steps if i % 2 == 0 else -steps)) % row_count) for i in range(row_count)]
        return lax.ppermute(value, "row", pairs)

    beside = swap(adjoint, 1)
    across = swap(adjoint, 2)
    chip = jnp.concatenate([adjoint, beside])
    far = to_plane(chip, 2, 0)
    across_near = to_plane(chip, 1, 2)
    near = to_plane(chip, 1, 0)
    wanted = [(i, i ^ 2) for i in range(row_count) if i % PLANE in (1, 2)]
    across_far = lax.ppermute(far, "row", wanted)

    groups = [list(range(half)), list(range(half, col_count))]
    wz = lax.all_to_all(wpart, "col", 0, 0, axis_index_groups=groups)
    halves = pl.pallas_call(
        halves_kernel,
        out_shape=jax.ShapeDtypeStruct((2 * feat, feat), BF),
        in_specs=[vmem()],
        out_specs=vmem(),
        compiler_params=small,
        name="halves",
    )(wz)

    def partner(value, axis, bit):
        return lax.ppermute(value, axis, [(i, i ^ bit) for i in range(lax.axis_size(axis))])

    received = jnp.concatenate([far, across_near, near, across, across_far, halves])
    other = swap(received, 1)

    sends, wsum = pl.pallas_call(
        tile_kernel,
        out_shape=(jax.ShapeDtypeStruct((col_count, nodes, feat), BF), jax.ShapeDtypeStruct((feat, feat), F32)),
        in_specs=[smem(), smem()] + [vmem()] * 5,
        out_specs=(pl.BlockSpec(memory_space=pl.ANY), vmem()),
        scratch_shapes=[
            pltpu.VMEM((20 * nodes, feat), BF),
            pltpu.VMEM((col_count * blocks_dev, SIDE, feat), F32),
            pltpu.VMEM((col_count, nodes, feat), BF),
            pltpu.SemaphoreType.DMA((col_count,)),
        ],
        compiler_params=params,
        cost_estimate=pl.CostEstimate(
            flops=2 * tiles * SIDE * SIDE * feat, bytes_accessed=6 << 20, transcendentals=0
        ),
        name="tiles",
    )(places, targets, tile_values, adjoint, beside, received, other)

    got = lax.all_to_all(sends, "col", 0, 0)
    for bit in [PLANE << k for k in range((row_count // PLANE - 1).bit_length())] + [2]:
        wsum = wsum + partner(wsum, "row", bit)
    wsum = wsum + partner(wsum, "col", half)
    scale = 1.0 / float(nodes * row_count * col_count) ** 0.5
    node_grad, weight_grad = pl.pallas_call(
        functools.partial(finish_kernel, scale),
        out_shape=(jax.ShapeDtypeStruct((nodes, feat), BF), jax.ShapeDtypeStruct((feat, feat), F32)),
        in_specs=[vmem(), vmem()],
        out_specs=(vmem(), vmem()),
        compiler_params=small,
        name="finish",
    )(got, wsum)
    return (node_grad, weight_grad)


def solution(mesh):
    split = P(("row", "col"))
    return jax.shard_map(
        on_device,
        mesh=mesh,
        in_specs=(split, split, split, P(), split, split, split, split),
        out_specs=(split, P()),
        check_vma=False,
    )
```

```python
import functools

import jax
import jax.numpy as jnp
from jax import lax
from jax.experimental import pallas as pl
from jax.experimental.pallas import tpu as pltpu
from jax.sharding import PartitionSpec as P

BF = jnp.bfloat16
F32 = jnp.float32
SIDE = 128
PLANE = 4


def dot(a, b, contract):
    return lax.dot_general(a, b, ((contract[:1], contract[1:]), ((), ())), preferred_element_type=F32)


def block_place(block, row, planes, cols, blocks):
    device = lax.div(block, blocks)
    group = lax.div(device, cols)
    gap = lax.rem(lax.div(group, PLANE) - lax.div(row, PLANE) + planes, planes)
    core = lax.rem(group, 2)
    same_core = core == lax.rem(row, 2)
    same_chip = lax.rem(lax.div(group, 2), 2) == lax.rem(lax.div(row, 2), 2)
    below = gap > planes // 2
    steps = jnp.where(below, planes - gap, gap)
    receiver = jnp.where(gap == 0, core, jnp.where(below, 0, 1))
    first = jnp.where(steps == 2, jnp.where(same_chip, 0, 6), jnp.where(same_chip, 2, 4))
    place = jnp.where(gap == 0, 8, first + jnp.where(core == receiver, 0, 1))
    slot = 2 + place + jnp.where(receiver == lax.rem(row, 2), 0, 9)
    slot = jnp.where((gap == 0) & same_chip, jnp.where(same_core, 0, 1), slot)
    return slot * blocks + lax.rem(block, blocks)


def adjoint_kernel(
    order_in, cot_in, pre_in, agg_in, w_in, in_in, to_in, out_ref, wpart_ref, place_ref, target_ref,
    order_ref, cot_ref, pre_ref, agg_ref, w_ref, in_ref, to_ref, sems,
):
    ins = (order_in, cot_in, pre_in, w_in, agg_in, in_in, to_in)
    held = (order_ref, cot_ref, pre_ref, w_ref, agg_ref, in_ref, to_ref)
    copies = [pltpu.make_async_copy(a, b, sems.at[i]) for i, (a, b) in enumerate(zip(ins, held))]
    for copy in copies:
        copy.start()
    for copy in copies:
        copy.wait()
    rows = cot_ref.shape[0]
    row, cols, blocks = lax.axis_index("row"), lax.axis_size("col"), rows // SIDE
    place_ref[...] = block_place(in_ref[...], row, lax.axis_size("row") // PLANE, cols, blocks) * SIDE
    target_ref[...] = to_ref[...] - row * cols * blocks
    cot = cot_ref[...]
    row_id = lax.broadcasted_iota(jnp.int32, (rows, SIDE), 0)
    base = (lax.axis_index("row") * lax.axis_size("col") + lax.axis_index("col")) * rows
    total = jnp.zeros(w_ref.shape, F32)
    for b in range(rows // SIDE):
        span = slice(b * SIDE, (b + 1) * SIDE)
        local = order_ref[b : b + 1, :] - base
        pick = jnp.where(row_id == local, 1.0, 0.0).astype(BF)
        grad_rows = dot(pick, cot, (0, 0))
        grad_pre = jnp.where(pre_ref[span, :].astype(F32) > 0, grad_rows, 0.0).astype(BF)
        total += dot(agg_ref[span, :], grad_pre, (0, 0))
        out_ref[span, :] = dot(grad_pre, w_ref[...], (1, 1)).astype(BF)
    for z in range(wpart_ref.shape[0]):
        wpart_ref[z] = total.astype(BF)


def halves_kernel(parts_ref, out_ref):
    total = parts_ref[0].astype(F32)
    for z in range(1, parts_ref.shape[0]):
        total += parts_ref[z].astype(F32)
    high = total.astype(BF)
    out_ref[: total.shape[0], :] = high
    out_ref[total.shape[0] :, :] = (total - high.astype(F32)).astype(BF)


def tile_kernel(
    from_ref, to_ref, tiles_ref, own, beside, ours, theirs, out_ref, weight_ref, blocks_ref, acc_ref, sent_ref, sems
):
    cols, rows, _ = out_ref.shape
    blocks = rows // SIDE
    feat = weight_ref.shape[0]
    sets = ours.shape[0] - 2 * feat
    at = 0
    for piece in (own[...], beside[...], ours[:sets, :], theirs[:sets, :]):
        blocks_ref[at : at + piece.shape[0], :] = piece
        at += piece.shape[0]
    acc_ref[...] = jnp.zeros_like(acc_ref)

    def one(t, carry):
        at = pl.multiple_of(from_ref[0, t], SIDE)
        acc_ref[to_ref[0, t]] += dot(tiles_ref[t], blocks_ref[pl.ds(at, SIDE), :], (1, 0))
        return carry

    lax.fori_loop(0, tiles_ref.shape[0], one, 0, unroll=8)
    copies = [pltpu.make_async_copy(sent_ref.at[c], out_ref.at[c], sems.at[c]) for c in range(cols)]
    for c in range(cols):
        for b in range(blocks):
            sent_ref[c, b * SIDE : (b + 1) * SIDE, :] = acc_ref[c * blocks + b].astype(BF)
        copies[c].start()
    mine, yours = [
        pair[sets : sets + feat, :].astype(F32) + pair[sets + feat :, :].astype(F32) for pair in (ours, theirs)
    ]
    weight_ref[...] = mine + yours
    for c in range(cols):
        copies[c].wait()


def finish_kernel(scale, got_ref, wsum_ref, out_ref, wgrad_ref):
    total = got_ref[0].astype(F32)
    for c in range(1, got_ref.shape[0]):
        total += got_ref[c].astype(F32)
    out_ref[...] = total.astype(BF)
    wgrad_ref[...] = wsum_ref[...] * scale


def vmem():
    return pl.BlockSpec(memory_space=pltpu.VMEM)


def smem():
    return pl.BlockSpec(memory_space=pltpu.SMEM)


def on_device(cotangent, pre_act, aggregated, weight, tile_values, tile_in, tile_out, order):
    row_count = lax.axis_size("row")
    col_count = lax.axis_size("col")
    nodes, feat = cotangent.shape
    blocks_dev = nodes // SIDE
    half = col_count // 2
    params = pltpu.CompilerParams(vmem_limit_bytes=12 << 20)
    small = pltpu.CompilerParams(vmem_limit_bytes=4 << 20)

    tiles = tile_values.shape[0]
    scalars = jax.ShapeDtypeStruct((1, tiles), jnp.int32)
    adjoint, wpart, places, targets = pl.pallas_call(
        adjoint_kernel,
        out_shape=(jax.ShapeDtypeStruct((nodes, feat), BF), jax.ShapeDtypeStruct((half, feat, feat), BF), scalars, scalars),
        in_specs=[pl.BlockSpec(memory_space=pltpu.HBM)] * 7,
        out_specs=(vmem(),) * 4,
        scratch_shapes=[
            pltpu.VMEM((blocks_dev, SIDE), jnp.int32),
            pltpu.VMEM((nodes, feat), BF),
            pltpu.VMEM((nodes, feat), BF),
            pltpu.VMEM((nodes, feat), BF),
            pltpu.VMEM((feat, feat), BF),
            pltpu.VMEM((1, tiles), jnp.int32),
            pltpu.VMEM((1, tiles), jnp.int32),
            pltpu.SemaphoreType.DMA((7,)),
        ],
        compiler_params=pltpu.CompilerParams(vmem_limit_bytes=60 << 20),
        name="adjoint",
    )(order.reshape(blocks_dev, SIDE), cotangent, pre_act, aggregated, weight, tile_in.reshape(1, tiles), tile_out.reshape(1, tiles))

    def swap(value, bit):
        return lax.ppermute(value, "row", [(i, i ^ bit) for i in range(row_count)])

    def to_plane(value, steps, chip_bit):
        pairs = [(i, ((i ^ chip_bit) + PLANE * (steps if i % 2 == 0 else -steps)) % row_count) for i in range(row_count)]
        return lax.ppermute(value, "row", pairs)

    beside = swap(adjoint, 1)
    across = swap(adjoint, 2)
    chip = jnp.concatenate([adjoint, beside])
    far = to_plane(chip, 2, 0)
    across_near = to_plane(chip, 1, 2)
    near = to_plane(chip, 1, 0)
    wanted = [(i, i ^ 2) for i in range(row_count) if i % PLANE in (1, 2)]
    across_far = lax.ppermute(far, "row", wanted)

    groups = [list(range(half)), list(range(half, col_count))]
    wz = lax.all_to_all(wpart, "col", 0, 0, axis_index_groups=groups)
    halves = pl.pallas_call(
        halves_kernel,
        out_shape=jax.ShapeDtypeStruct((2 * feat, feat), BF),
        in_specs=[vmem()],
        out_specs=vmem(),
        compiler_params=small,
        name="halves",
    )(wz)

    def partner(value, axis, bit):
        return lax.ppermute(value, axis, [(i, i ^ bit) for i in range(lax.axis_size(axis))])

    received = jnp.concatenate([far, near, across_near, across_far, across, halves])
    other = swap(received, 1)

    sends, wsum = pl.pallas_call(
        tile_kernel,
        out_shape=(jax.ShapeDtypeStruct((col_count, nodes, feat), BF), jax.ShapeDtypeStruct((feat, feat), F32)),
        in_specs=[smem(), smem()] + [vmem()] * 5,
        out_specs=(pl.BlockSpec(memory_space=pl.ANY), vmem()),
        scratch_shapes=[
            pltpu.VMEM((20 * nodes, feat), BF),
            pltpu.VMEM((col_count * blocks_dev, SIDE, feat), F32),
            pltpu.VMEM((col_count, nodes, feat), BF),
            pltpu.SemaphoreType.DMA((col_count,)),
        ],
        compiler_params=params,
        cost_estimate=pl.CostEstimate(
            flops=2 * tiles * SIDE * SIDE * feat, bytes_accessed=6 << 20, transcendentals=0
        ),
        name="tiles",
    )(places, targets, tile_values, adjoint, beside, received, other)

    got = lax.all_to_all(sends, "col", 0, 0)
    for bit in [PLANE << k for k in range((row_count // PLANE - 1).bit_length())] + [2]:
        wsum = wsum + partner(wsum, "row", bit)
    wsum = wsum + partner(wsum, "col", half)
    scale = 1.0 / float(nodes * row_count * col_count) ** 0.5
    node_grad, weight_grad = pl.pallas_call(
        functools.partial(finish_kernel, scale),
        out_shape=(jax.ShapeDtypeStruct((nodes, feat), BF), jax.ShapeDtypeStruct((feat, feat), F32)),
        in_specs=[vmem(), vmem()],
        out_specs=(vmem(), vmem()),
        compiler_params=small,
        name="finish",
    )(got, wsum)
    return (node_grad, weight_grad)


def solution(mesh):
    split = P(("row", "col"))
    return jax.shard_map(
        on_device,
        mesh=mesh,
        in_specs=(split, split, split, P(), split, split, split, split),
        out_specs=(split, P()),
        check_vma=False,
    )
```

```python
import functools

import jax
import jax.numpy as jnp
from jax import lax
from jax.experimental import pallas as pl
from jax.experimental.pallas import tpu as pltpu
from jax.sharding import PartitionSpec as P

BF = jnp.bfloat16
F32 = jnp.float32
SIDE = 128
PLANE = 4


def dot(a, b, contract):
    return lax.dot_general(a, b, ((contract[:1], contract[1:]), ((), ())), preferred_element_type=F32)


def block_place(block, row, planes, cols, blocks):
    device = lax.div(block, blocks)
    group = lax.div(device, cols)
    gap = lax.rem(lax.div(group, PLANE) - lax.div(row, PLANE) + planes, planes)
    core = lax.rem(group, 2)
    same_core = core == lax.rem(row, 2)
    same_chip = lax.rem(lax.div(group, 2), 2) == lax.rem(lax.div(row, 2), 2)
    below = gap > planes // 2
    steps = jnp.where(below, planes - gap, gap)
    receiver = jnp.where(gap == 0, 1 - core, jnp.where(below, 0, 1))
    first = jnp.where(steps == 2, jnp.where(same_chip, 2, 4), jnp.where(same_chip, 0, 7))
    place = jnp.where(gap == 0, 6, first + jnp.where(core == receiver, 0, 1))
    slot = 2 + place + jnp.where(receiver == lax.rem(row, 2), 0, 9)
    slot = jnp.where((gap == 0) & same_chip, jnp.where(same_core, 0, 1), slot)
    return slot * blocks + lax.rem(block, blocks)


def adjoint_kernel(
    order_in, cot_in, pre_in, agg_in, w_in, in_in, to_in, out_ref, wpart_ref, place_ref, target_ref,
    order_ref, cot_ref, pre_ref, agg_ref, w_ref, in_ref, to_ref, sems,
):
    ins = (order_in, cot_in, pre_in, w_in, agg_in, in_in, to_in)
    held = (order_ref, cot_ref, pre_ref, w_ref, agg_ref, in_ref, to_ref)
    copies = [pltpu.make_async_copy(a, b, sems.at[i]) for i, (a, b) in enumerate(zip(ins, held))]
    for copy in copies:
        copy.start()
    for copy in copies:
        copy.wait()
    rows = cot_ref.shape[0]
    row, cols, blocks = lax.axis_index("row"), lax.axis_size("col"), rows // SIDE
    place_ref[...] = block_place(in_ref[...], row, lax.axis_size("row") // PLANE, cols, blocks) * SIDE
    target_ref[...] = to_ref[...] - row * cols * blocks
    cot = cot_ref[...]
    row_id = lax.broadcasted_iota(jnp.int32, (rows, SIDE), 0)
    base = (lax.axis_index("row") * lax.axis_size("col") + lax.axis_index("col")) * rows
    total = jnp.zeros(w_ref.shape, F32)
    for b in range(rows // SIDE):
        span = slice(b * SIDE, (b + 1) * SIDE)
        local = order_ref[b : b + 1, :] - base
        pick = jnp.where(row_id == local, 1.0, 0.0).astype(BF)
        grad_rows = dot(pick, cot, (0, 0))
        grad_pre = jnp.where(pre_ref[span, :].astype(F32) > 0, grad_rows, 0.0).astype(BF)
        total += dot(agg_ref[span, :], grad_pre, (0, 0))
        out_ref[span, :] = dot(grad_pre, w_ref[...], (1, 1)).astype(BF)
    for z in range(wpart_ref.shape[0]):
        wpart_ref[z] = total.astype(BF)


def halves_kernel(parts_ref, out_ref):
    total = parts_ref[0].astype(F32)
    for z in range(1, parts_ref.shape[0]):
        total += parts_ref[z].astype(F32)
    high = total.astype(BF)
    out_ref[: total.shape[0], :] = high
    out_ref[total.shape[0] :, :] = (total - high.astype(F32)).astype(BF)


def tile_kernel(
    from_ref, to_ref, tiles_ref, own, beside, ours, theirs, out_ref, weight_ref, blocks_ref, acc_ref, sent_ref, sems
):
    cols, rows, _ = out_ref.shape
    blocks = rows // SIDE
    feat = weight_ref.shape[0]
    sets = ours.shape[0] - 2 * feat
    at = 0
    for piece in (own[...], beside[...], ours[:sets, :], theirs[:sets, :]):
        blocks_ref[at : at + piece.shape[0], :] = piece
        at += piece.shape[0]
    acc_ref[...] = jnp.zeros_like(acc_ref)

    def one(t, carry):
        at = pl.multiple_of(from_ref[0, t], SIDE)
        acc_ref[to_ref[0, t]] += dot(tiles_ref[t], blocks_ref[pl.ds(at, SIDE), :], (1, 0))
        return carry

    lax.fori_loop(0, tiles_ref.shape[0], one, 0, unroll=8)
    copies = [pltpu.make_async_copy(sent_ref.at[c], out_ref.at[c], sems.at[c]) for c in range(cols)]
    for c in range(cols):
        for b in range(blocks):
            sent_ref[c, b * SIDE : (b + 1) * SIDE, :] = acc_ref[c * blocks + b].astype(BF)
        copies[c].start()
    mine, yours = [
        pair[sets : sets + feat, :].astype(F32) + pair[sets + feat :, :].astype(F32) for pair in (ours, theirs)
    ]
    weight_ref[...] = mine + yours
    for c in range(cols):
        copies[c].wait()


def finish_kernel(scale, got_ref, wsum_ref, out_ref, wgrad_ref):
    total = got_ref[0].astype(F32)
    for c in range(1, got_ref.shape[0]):
        total += got_ref[c].astype(F32)
    out_ref[...] = total.astype(BF)
    wgrad_ref[...] = wsum_ref[...] * scale


def vmem():
    return pl.BlockSpec(memory_space=pltpu.VMEM)


def smem():
    return pl.BlockSpec(memory_space=pltpu.SMEM)


def on_device(cotangent, pre_act, aggregated, weight, tile_values, tile_in, tile_out, order):
    row_count = lax.axis_size("row")
    col_count = lax.axis_size("col")
    nodes, feat = cotangent.shape
    blocks_dev = nodes // SIDE
    half = col_count // 2
    params = pltpu.CompilerParams(vmem_limit_bytes=12 << 20)
    small = pltpu.CompilerParams(vmem_limit_bytes=4 << 20)

    tiles = tile_values.shape[0]
    scalars = jax.ShapeDtypeStruct((1, tiles), jnp.int32)
    adjoint, wpart, places, targets = pl.pallas_call(
        adjoint_kernel,
        out_shape=(jax.ShapeDtypeStruct((nodes, feat), BF), jax.ShapeDtypeStruct((half, feat, feat), BF), scalars, scalars),
        in_specs=[pl.BlockSpec(memory_space=pltpu.HBM)] * 7,
        out_specs=(vmem(),) * 4,
        scratch_shapes=[
            pltpu.VMEM((blocks_dev, SIDE), jnp.int32),
            pltpu.VMEM((nodes, feat), BF),
            pltpu.VMEM((nodes, feat), BF),
            pltpu.VMEM((nodes, feat), BF),
            pltpu.VMEM((feat, feat), BF),
            pltpu.VMEM((1, tiles), jnp.int32),
            pltpu.VMEM((1, tiles), jnp.int32),
            pltpu.SemaphoreType.DMA((7,)),
        ],
        compiler_params=pltpu.CompilerParams(vmem_limit_bytes=60 << 20),
        name="adjoint",
    )(order.reshape(blocks_dev, SIDE), cotangent, pre_act, aggregated, weight, tile_in.reshape(1, tiles), tile_out.reshape(1, tiles))

    def swap(value, bit):
        return lax.ppermute(value, "row", [(i, i ^ bit) for i in range(row_count)])

    def to_plane(value, steps, chip_bit, wanted):
        pairs = [(i, ((i ^ chip_bit) + PLANE * (steps if i % 2 == 0 else -steps)) % row_count) for i in range(row_count)]
        return lax.ppermute(value, "row", [pair for pair in pairs if pair[0] % PLANE in wanted])

    beside = swap(adjoint, 1)
    chip = jnp.concatenate([adjoint, beside])
    near = to_plane(chip, 1, 0, (0, 1, 2, 3))
    far = to_plane(chip, 2, 0, (0, 1, 2, 3))
    across_far = to_plane(chip, 2, 2, (1, 2))
    across = swap(jnp.concatenate([beside, near]), 2)

    groups = [list(range(half)), list(range(half, col_count))]
    wz = lax.all_to_all(wpart, "col", 0, 0, axis_index_groups=groups)
    halves = pl.pallas_call(
        halves_kernel,
        out_shape=jax.ShapeDtypeStruct((2 * feat, feat), BF),
        in_specs=[vmem()],
        out_specs=vmem(),
        compiler_params=small,
        name="halves",
    )(wz)

    def partner(value, axis, bit):
        return lax.ppermute(value, axis, [(i, i ^ bit) for i in range(lax.axis_size(axis))])

    received = jnp.concatenate([near, far, across_far, across, halves])
    other = swap(received, 1)

    sends, wsum = pl.pallas_call(
        tile_kernel,
        out_shape=(jax.ShapeDtypeStruct((col_count, nodes, feat), BF), jax.ShapeDtypeStruct((feat, feat), F32)),
        in_specs=[smem(), smem()] + [vmem()] * 5,
        out_specs=(pl.BlockSpec(memory_space=pl.ANY), vmem()),
        scratch_shapes=[
            pltpu.VMEM((20 * nodes, feat), BF),
            pltpu.VMEM((col_count * blocks_dev, SIDE, feat), F32),
            pltpu.VMEM((col_count, nodes, feat), BF),
            pltpu.SemaphoreType.DMA((col_count,)),
        ],
        compiler_params=params,
        cost_estimate=pl.CostEstimate(
            flops=2 * tiles * SIDE * SIDE * feat, bytes_accessed=6 << 20, transcendentals=0
        ),
        name="tiles",
    )(places, targets, tile_values, adjoint, beside, received, other)

    got = lax.all_to_all(sends, "col", 0, 0)
    for bit in [PLANE << k for k in range((row_count // PLANE - 1).bit_length())] + [2]:
        wsum = wsum + partner(wsum, "row", bit)
    wsum = wsum + partner(wsum, "col", half)
    scale = 1.0 / float(nodes * row_count * col_count) ** 0.5
    node_grad, weight_grad = pl.pallas_call(
        functools.partial(finish_kernel, scale),
        out_shape=(jax.ShapeDtypeStruct((nodes, feat), BF), jax.ShapeDtypeStruct((feat, feat), F32)),
        in_specs=[vmem(), vmem()],
        out_specs=(vmem(), vmem()),
        compiler_params=small,
        name="finish",
    )(got, wsum)
    return (node_grad, weight_grad)


def solution(mesh):
    split = P(("row", "col"))
    return jax.shard_map(
        on_device,
        mesh=mesh,
        in_specs=(split, split, split, P(), split, split, split, split),
        out_specs=(split, P()),
        check_vma=False,
    )
```

```python
import functools

import jax
import jax.numpy as jnp
from jax import lax
from jax.experimental import pallas as pl
from jax.experimental.pallas import tpu as pltpu
from jax.sharding import PartitionSpec as P

BF = jnp.bfloat16
F32 = jnp.float32
SIDE = 128
PLANE = 4


def dot(a, b, contract):
    return lax.dot_general(a, b, ((contract[:1], contract[1:]), ((), ())), preferred_element_type=F32)


def block_place(block, row, planes, cols, blocks):
    device = lax.div(block, blocks)
    group = lax.div(device, cols)
    gap = lax.rem(lax.div(group, PLANE) - lax.div(row, PLANE) + planes, planes)
    core = lax.rem(group, 2)
    same_core = core == lax.rem(row, 2)
    same_chip = lax.rem(lax.div(group, 2), 2) == lax.rem(lax.div(row, 2), 2)
    below = gap > planes // 2
    steps = jnp.where(below, planes - gap, gap)
    receiver = jnp.where(gap == 0, 1 - core, jnp.where(below, 0, 1))
    first = jnp.where(steps == 2, jnp.where(same_chip, 2, 4), jnp.where(same_chip, 0, 7))
    place = jnp.where(gap == 0, 6, first + jnp.where(core == receiver, 0, 1))
    slot = 2 + place + jnp.where(receiver == lax.rem(row, 2), 0, 9)
    slot = jnp.where((gap == 0) & same_chip, jnp.where(same_core, 0, 1), slot)
    return slot * blocks + lax.rem(block, blocks)


def adjoint_kernel(
    order_in, cot_in, pre_in, agg_in, w_in, in_in, to_in, out_ref, wpart_ref, place_ref, target_ref,
    order_ref, cot_ref, pre_ref, agg_ref, w_ref, in_ref, to_ref, sems,
):
    ins = (order_in, cot_in, pre_in, w_in, agg_in, in_in, to_in)
    held = (order_ref, cot_ref, pre_ref, w_ref, agg_ref, in_ref, to_ref)
    copies = [pltpu.make_async_copy(a, b, sems.at[i]) for i, (a, b) in enumerate(zip(ins, held))]
    for copy in copies:
        copy.start()
    for copy in copies:
        copy.wait()
    rows = cot_ref.shape[0]
    row, cols, blocks = lax.axis_index("row"), lax.axis_size("col"), rows // SIDE
    place_ref[...] = block_place(in_ref[...], row, lax.axis_size("row") // PLANE, cols, blocks) * SIDE
    target_ref[...] = to_ref[...] - row * cols * blocks
    cot = cot_ref[...]
    row_id = lax.broadcasted_iota(jnp.int32, (rows, SIDE), 0)
    base = (lax.axis_index("row") * lax.axis_size("col") + lax.axis_index("col")) * rows
    total = jnp.zeros(w_ref.shape, F32)
    for b in range(rows // SIDE):
        span = slice(b * SIDE, (b + 1) * SIDE)
        local = order_ref[b : b + 1, :] - base
        pick = jnp.where(row_id == local, 1.0, 0.0).astype(BF)
        grad_rows = dot(pick, cot, (0, 0))
        grad_pre = jnp.where(pre_ref[span, :].astype(F32) > 0, grad_rows, 0.0).astype(BF)
        total += dot(agg_ref[span, :], grad_pre, (0, 0))
        out_ref[span, :] = dot(grad_pre, w_ref[...], (1, 1)).astype(BF)
    for z in range(wpart_ref.shape[0]):
        wpart_ref[z] = total.astype(BF)


def halves_kernel(parts_ref, out_ref):
    total = parts_ref[0].astype(F32)
    for z in range(1, parts_ref.shape[0]):
        total += parts_ref[z].astype(F32)
    high = total.astype(BF)
    out_ref[: total.shape[0], :] = high
    out_ref[total.shape[0] :, :] = (total - high.astype(F32)).astype(BF)


def tile_kernel(
    from_ref, to_ref, tiles_ref, own, beside, ours, theirs, out_ref, weight_ref, blocks_ref, acc_ref, sent_ref, sems
):
    cols, rows, _ = out_ref.shape
    blocks = rows // SIDE
    feat = weight_ref.shape[0]
    sets = ours.shape[0] - 2 * feat
    at = 0
    for piece in (own[...], beside[...], ours[:sets, :], theirs[:sets, :]):
        blocks_ref[at : at + piece.shape[0], :] = piece
        at += piece.shape[0]
    acc_ref[...] = jnp.zeros_like(acc_ref)

    def one(t, carry):
        at = pl.multiple_of(from_ref[0, t], SIDE)
        acc_ref[to_ref[0, t]] += dot(tiles_ref[t], blocks_ref[pl.ds(at, SIDE), :], (1, 0))
        return carry

    lax.fori_loop(0, tiles_ref.shape[0], one, 0, unroll=8)
    copies = [pltpu.make_async_copy(sent_ref.at[c], out_ref.at[c], sems.at[c]) for c in range(cols)]
    for c in range(cols):
        for b in range(blocks):
            sent_ref[c, b * SIDE : (b + 1) * SIDE, :] = acc_ref[c * blocks + b].astype(BF)
        copies[c].start()
    mine, yours = [
        pair[sets : sets + feat, :].astype(F32) + pair[sets + feat :, :].astype(F32) for pair in (ours, theirs)
    ]
    weight_ref[...] = mine + yours
    for c in range(cols):
        copies[c].wait()


def finish_kernel(scale, got_ref, wsum_ref, out_ref, wgrad_ref):
    total = got_ref[0].astype(F32)
    for c in range(1, got_ref.shape[0]):
        total += got_ref[c].astype(F32)
    out_ref[...] = total.astype(BF)
    wgrad_ref[...] = wsum_ref[...] * scale


def vmem():
    return pl.BlockSpec(memory_space=pltpu.VMEM)


def smem():
    return pl.BlockSpec(memory_space=pltpu.SMEM)


def on_device(cotangent, pre_act, aggregated, weight, tile_values, tile_in, tile_out, order):
    row_count = lax.axis_size("row")
    col_count = lax.axis_size("col")
    nodes, feat = cotangent.shape
    blocks_dev = nodes // SIDE
    half = col_count // 2
    params = pltpu.CompilerParams(vmem_limit_bytes=12 << 20)
    small = pltpu.CompilerParams(vmem_limit_bytes=4 << 20)

    tiles = tile_values.shape[0]
    scalars = jax.ShapeDtypeStruct((1, tiles), jnp.int32)
    adjoint, wpart, places, targets = pl.pallas_call(
        adjoint_kernel,
        out_shape=(jax.ShapeDtypeStruct((nodes, feat), BF), jax.ShapeDtypeStruct((half, feat, feat), BF), scalars, scalars),
        in_specs=[pl.BlockSpec(memory_space=pltpu.HBM)] * 7,
        out_specs=(vmem(),) * 4,
        scratch_shapes=[
            pltpu.VMEM((blocks_dev, SIDE), jnp.int32),
            pltpu.VMEM((nodes, feat), BF),
            pltpu.VMEM((nodes, feat), BF),
            pltpu.VMEM((nodes, feat), BF),
            pltpu.VMEM((feat, feat), BF),
            pltpu.VMEM((1, tiles), jnp.int32),
            pltpu.VMEM((1, tiles), jnp.int32),
            pltpu.SemaphoreType.DMA((7,)),
        ],
        compiler_params=pltpu.CompilerParams(vmem_limit_bytes=60 << 20),
        name="adjoint",
    )(order.reshape(blocks_dev, SIDE), cotangent, pre_act, aggregated, weight, tile_in.reshape(1, tiles), tile_out.reshape(1, tiles))

    def swap(value, bit):
        return lax.ppermute(value, "row", [(i, i ^ bit) for i in range(row_count)])

    def to_plane(value, steps, chip_bit, wanted):
        pairs = [(i, ((i ^ chip_bit) + PLANE * (steps if i % 2 == 0 else -steps)) % row_count) for i in range(row_count)]
        return lax.ppermute(value, "row", [pair for pair in pairs if pair[0] % PLANE in wanted])

    beside = swap(adjoint, 1)
    chip = jnp.concatenate([adjoint, beside])
    near = to_plane(chip, 1, 0, (0, 1, 2, 3))
    far = to_plane(chip, 2, 0, (0, 1, 2, 3))
    across_far = to_plane(chip, 2, 2, (1, 2))
    across = swap(jnp.concatenate([beside, near]), 2)

    groups = [list(range(half)), list(range(half, col_count))]
    wz = lax.all_to_all(wpart, "col", 0, 0, axis_index_groups=groups)
    halves = pl.pallas_call(
        halves_kernel,
        out_shape=jax.ShapeDtypeStruct((2 * feat, feat), BF),
        in_specs=[vmem()],
        out_specs=vmem(),
        compiler_params=small,
        name="halves",
    )(wz)

    def partner(value, axis, bit):
        return lax.ppermute(value, axis, [(i, i ^ bit) for i in range(lax.axis_size(axis))])

    received = jnp.concatenate([near, far, across_far, across, halves])
    other = swap(received, 1)

    sends, wsum = pl.pallas_call(
        tile_kernel,
        out_shape=(jax.ShapeDtypeStruct((col_count, nodes, feat), BF), jax.ShapeDtypeStruct((feat, feat), F32)),
        in_specs=[smem(), smem()] + [vmem()] * 5,
        out_specs=(pl.BlockSpec(memory_space=pl.ANY), vmem()),
        scratch_shapes=[
            pltpu.VMEM((20 * nodes, feat), BF),
            pltpu.VMEM((col_count * blocks_dev, SIDE, feat), F32),
            pltpu.VMEM((col_count, nodes, feat), BF),
            pltpu.SemaphoreType.DMA((col_count,)),
        ],
        compiler_params=params,
        cost_estimate=pl.CostEstimate(
            flops=2 * tiles * SIDE * SIDE * feat, bytes_accessed=6 << 20, transcendentals=0
        ),
        name="tiles",
    )(places, targets, tile_values, adjoint, beside, received, other)

    got = lax.all_to_all(sends, "col", 0, 0)
    planes = row_count // PLANE
    for bit in [PLANE << k for k in range((planes - 1).bit_length() - 1)]:
        wsum = wsum + partner(wsum, "row", bit)
    mirrored = [(i, (planes - 1 - i // PLANE) * PLANE + i % PLANE) for i in range(row_count)]
    wsum = wsum + lax.ppermute(wsum, "row", mirrored)
    wsum = wsum + partner(wsum, "row", 2)
    spots = [(r, c) for r in range(row_count) for c in range(col_count)]
    facing = [(r * col_count + c, (r ^ 2) * col_count + (c + half) % col_count) for r, c in spots]
    wsum = wsum + lax.ppermute(wsum, ("row", "col"), facing)
    scale = 1.0 / float(nodes * row_count * col_count) ** 0.5
    node_grad, weight_grad = pl.pallas_call(
        functools.partial(finish_kernel, scale),
        out_shape=(jax.ShapeDtypeStruct((nodes, feat), BF), jax.ShapeDtypeStruct((feat, feat), F32)),
        in_specs=[vmem(), vmem()],
        out_specs=(vmem(), vmem()),
        compiler_params=small,
        name="finish",
    )(got, wsum)
    return (node_grad, weight_grad)


def solution(mesh):
    split = P(("row", "col"))
    return jax.shard_map(
        on_device,
        mesh=mesh,
        in_specs=(split, split, split, P(), split, split, split, split),
        out_specs=(split, P()),
        check_vma=False,
    )
```

```python
import functools

import jax
import jax.numpy as jnp
from jax import lax
from jax.experimental import pallas as pl
from jax.experimental.pallas import tpu as pltpu
from jax.sharding import PartitionSpec as P

BF = jnp.bfloat16
F32 = jnp.float32
SIDE = 128
PLANE = 4


def dot(a, b, contract):
    return lax.dot_general(a, b, ((contract[:1], contract[1:]), ((), ())), preferred_element_type=F32)


def block_place(block, row, planes, cols, blocks):
    device = lax.div(block, blocks)
    group = lax.div(device, cols)
    gap = lax.rem(lax.div(group, PLANE) - lax.div(row, PLANE) + planes, planes)
    core = lax.rem(group, 2)
    same_core = core == lax.rem(row, 2)
    same_chip = lax.rem(lax.div(group, 2), 2) == lax.rem(lax.div(row, 2), 2)
    below = gap > planes // 2
    steps = jnp.where(below, planes - gap, gap)
    receiver = jnp.where(gap == 0, 1 - core, jnp.where(below, 0, 1))
    first = jnp.where(steps == 2, jnp.where(same_chip, 7, 5), jnp.where(same_chip, 0, 3))
    place = jnp.where(gap == 0, 2, first + jnp.where(core == receiver, 0, 1))
    slot = 2 + place + jnp.where(receiver == lax.rem(row, 2), 0, 9)
    slot = jnp.where((gap == 0) & same_chip, jnp.where(same_core, 0, 1), slot)
    return slot * blocks + lax.rem(block, blocks)


def adjoint_kernel(
    order_in, cot_in, pre_in, agg_in, w_in, in_in, to_in, out_ref, wpart_ref, place_ref, target_ref,
    order_ref, cot_ref, pre_ref, agg_ref, w_ref, in_ref, to_ref, sems,
):
    ins = (order_in, cot_in, pre_in, w_in, agg_in, in_in, to_in)
    held = (order_ref, cot_ref, pre_ref, w_ref, agg_ref, in_ref, to_ref)
    copies = [pltpu.make_async_copy(a, b, sems.at[i]) for i, (a, b) in enumerate(zip(ins, held))]
    for copy in copies:
        copy.start()
    for copy in copies:
        copy.wait()
    rows = cot_ref.shape[0]
    row, cols, blocks = lax.axis_index("row"), lax.axis_size("col"), rows // SIDE
    place_ref[...] = block_place(in_ref[...], row, lax.axis_size("row") // PLANE, cols, blocks) * SIDE
    target_ref[...] = to_ref[...] - row * cols * blocks
    cot = cot_ref[...]
    row_id = lax.broadcasted_iota(jnp.int32, (rows, SIDE), 0)
    base = (lax.axis_index("row") * lax.axis_size("col") + lax.axis_index("col")) * rows
    total = jnp.zeros(w_ref.shape, F32)
    for b in range(rows // SIDE):
        span = slice(b * SIDE, (b + 1) * SIDE)
        local = order_ref[b : b + 1, :] - base
        pick = jnp.where(row_id == local, 1.0, 0.0).astype(BF)
        grad_rows = dot(pick, cot, (0, 0))
        grad_pre = jnp.where(pre_ref[span, :].astype(F32) > 0, grad_rows, 0.0).astype(BF)
        total += dot(agg_ref[span, :], grad_pre, (0, 0))
        out_ref[span, :] = dot(grad_pre, w_ref[...], (1, 1)).astype(BF)
    for z in range(wpart_ref.shape[0]):
        wpart_ref[z] = total.astype(BF)


def halves_kernel(parts_ref, out_ref):
    total = parts_ref[0].astype(F32)
    for z in range(1, parts_ref.shape[0]):
        total += parts_ref[z].astype(F32)
    high = total.astype(BF)
    out_ref[: total.shape[0], :] = high
    out_ref[total.shape[0] :, :] = (total - high.astype(F32)).astype(BF)


def tile_kernel(
    from_ref, to_ref, tiles_ref, own, beside, ours, theirs, out_ref, weight_ref, blocks_ref, acc_ref, sent_ref, sems
):
    cols, rows, _ = out_ref.shape
    blocks = rows // SIDE
    feat = weight_ref.shape[0]
    sets = ours.shape[0] - 2 * feat
    at = 0
    for piece in (own[...], beside[...], ours[:sets, :], theirs[:sets, :]):
        blocks_ref[at : at + piece.shape[0], :] = piece
        at += piece.shape[0]
    acc_ref[...] = jnp.zeros_like(acc_ref)

    def one(t, carry):
        at = pl.multiple_of(from_ref[0, t], SIDE)
        acc_ref[to_ref[0, t]] += dot(tiles_ref[t], blocks_ref[pl.ds(at, SIDE), :], (1, 0))
        return carry

    lax.fori_loop(0, tiles_ref.shape[0], one, 0, unroll=8)
    copies = [pltpu.make_async_copy(sent_ref.at[c], out_ref.at[c], sems.at[c]) for c in range(cols)]
    for c in range(cols):
        for b in range(blocks):
            sent_ref[c, b * SIDE : (b + 1) * SIDE, :] = acc_ref[c * blocks + b].astype(BF)
        copies[c].start()
    mine, yours = [
        pair[sets : sets + feat, :].astype(F32) + pair[sets + feat :, :].astype(F32) for pair in (ours, theirs)
    ]
    weight_ref[...] = mine + yours
    for c in range(cols):
        copies[c].wait()


def finish_kernel(scale, got_ref, wsum_ref, out_ref, wgrad_ref):
    total = got_ref[0].astype(F32)
    for c in range(1, got_ref.shape[0]):
        total += got_ref[c].astype(F32)
    out_ref[...] = total.astype(BF)
    wgrad_ref[...] = wsum_ref[...] * scale


def vmem():
    return pl.BlockSpec(memory_space=pltpu.VMEM)


def smem():
    return pl.BlockSpec(memory_space=pltpu.SMEM)


def on_device(cotangent, pre_act, aggregated, weight, tile_values, tile_in, tile_out, order):
    row_count = lax.axis_size("row")
    col_count = lax.axis_size("col")
    nodes, feat = cotangent.shape
    blocks_dev = nodes // SIDE
    half = col_count // 2
    params = pltpu.CompilerParams(vmem_limit_bytes=12 << 20)
    small = pltpu.CompilerParams(vmem_limit_bytes=4 << 20)

    tiles = tile_values.shape[0]
    scalars = jax.ShapeDtypeStruct((1, tiles), jnp.int32)
    adjoint, wpart, places, targets = pl.pallas_call(
        adjoint_kernel,
        out_shape=(jax.ShapeDtypeStruct((nodes, feat), BF), jax.ShapeDtypeStruct((half, feat, feat), BF), scalars, scalars),
        in_specs=[pl.BlockSpec(memory_space=pltpu.HBM)] * 7,
        out_specs=(vmem(),) * 4,
        scratch_shapes=[
            pltpu.VMEM((blocks_dev, SIDE), jnp.int32),
            pltpu.VMEM((nodes, feat), BF),
            pltpu.VMEM((nodes, feat), BF),
            pltpu.VMEM((nodes, feat), BF),
            pltpu.VMEM((feat, feat), BF),
            pltpu.VMEM((1, tiles), jnp.int32),
            pltpu.VMEM((1, tiles), jnp.int32),
            pltpu.SemaphoreType.DMA((7,)),
        ],
        compiler_params=pltpu.CompilerParams(vmem_limit_bytes=60 << 20),
        name="adjoint",
    )(order.reshape(blocks_dev, SIDE), cotangent, pre_act, aggregated, weight, tile_in.reshape(1, tiles), tile_out.reshape(1, tiles))

    def swap(value, bit):
        return lax.ppermute(value, "row", [(i, i ^ bit) for i in range(row_count)])

    def to_plane(value, steps, chip_bit, wanted):
        pairs = [(i, ((i ^ chip_bit) + PLANE * (steps if i % 2 == 0 else -steps)) % row_count) for i in range(row_count)]
        return lax.ppermute(value, "row", [pair for pair in pairs if pair[0] % PLANE in wanted])

    beside = swap(adjoint, 1)
    chip = jnp.concatenate([adjoint, beside])
    near = to_plane(chip, 1, 0, (0, 1, 2, 3))
    far = to_plane(chip, 2, 0, (0, 1, 2, 3))
    across_far = to_plane(chip, 2, 2, (1, 2))
    across = swap(jnp.concatenate([beside, near]), 2)

    groups = [list(range(half)), list(range(half, col_count))]
    wz = lax.all_to_all(wpart, "col", 0, 0, axis_index_groups=groups)
    halves = pl.pallas_call(
        halves_kernel,
        out_shape=jax.ShapeDtypeStruct((2 * feat, feat), BF),
        in_specs=[vmem()],
        out_specs=vmem(),
        compiler_params=small,
        name="halves",
    )(wz)

    def partner(value, axis, bit):
        return lax.ppermute(value, axis, [(i, i ^ bit) for i in range(lax.axis_size(axis))])

    received = jnp.concatenate([near, across, across_far, far, halves])
    other = swap(received, 1)

    sends, wsum = pl.pallas_call(
        tile_kernel,
        out_shape=(jax.ShapeDtypeStruct((col_count, nodes, feat), BF), jax.ShapeDtypeStruct((feat, feat), F32)),
        in_specs=[smem(), smem()] + [vmem()] * 5,
        out_specs=(pl.BlockSpec(memory_space=pl.ANY), vmem()),
        scratch_shapes=[
            pltpu.VMEM((20 * nodes, feat), BF),
            pltpu.VMEM((col_count * blocks_dev, SIDE, feat), F32),
            pltpu.VMEM((col_count, nodes, feat), BF),
            pltpu.SemaphoreType.DMA((col_count,)),
        ],
        compiler_params=params,
        cost_estimate=pl.CostEstimate(
            flops=2 * tiles * SIDE * SIDE * feat, bytes_accessed=6 << 20, transcendentals=0
        ),
        name="tiles",
    )(places, targets, tile_values, adjoint, beside, received, other)

    got = lax.all_to_all(sends, "col", 0, 0)
    planes = row_count // PLANE
    for bit in [PLANE << k for k in range((planes - 1).bit_length() - 1)]:
        wsum = wsum + partner(wsum, "row", bit)
    mirrored = [(i, (planes - 1 - i // PLANE) * PLANE + i % PLANE) for i in range(row_count)]
    wsum = wsum + lax.ppermute(wsum, "row", mirrored)
    wsum = wsum + partner(wsum, "row", 2)
    spots = [(r, c) for r in range(row_count) for c in range(col_count)]
    facing = [(r * col_count + c, (r ^ 2) * col_count + (c + half) % col_count) for r, c in spots]
    wsum = wsum + lax.ppermute(wsum, ("row", "col"), facing)
    scale = 1.0 / float(nodes * row_count * col_count) ** 0.5
    node_grad, weight_grad = pl.pallas_call(
        functools.partial(finish_kernel, scale),
        out_shape=(jax.ShapeDtypeStruct((nodes, feat), BF), jax.ShapeDtypeStruct((feat, feat), F32)),
        in_specs=[vmem(), vmem()],
        out_specs=(vmem(), vmem()),
        compiler_params=small,
        name="finish",
    )(got, wsum)
    return (node_grad, weight_grad)


def solution(mesh):
    split = P(("row", "col"))
    return jax.shard_map(
        on_device,
        mesh=mesh,
        in_specs=(split, split, split, P(), split, split, split, split),
        out_specs=(split, P()),
        check_vma=False,
    )
```

```python
import functools

import jax
import jax.numpy as jnp
from jax import lax
from jax.experimental import pallas as pl
from jax.experimental.pallas import tpu as pltpu
from jax.sharding import PartitionSpec as P

BF = jnp.bfloat16
F32 = jnp.float32
SIDE = 128
PLANE = 4


def dot(a, b, contract):
    return lax.dot_general(a, b, ((contract[:1], contract[1:]), ((), ())), preferred_element_type=F32)


def block_place(block, row, planes, cols, blocks):
    device = lax.div(block, blocks)
    group = lax.div(device, cols)
    gap = lax.rem(lax.div(group, PLANE) - lax.div(row, PLANE) + planes, planes)
    core = lax.rem(group, 2)
    same_core = core == lax.rem(row, 2)
    same_chip = lax.rem(lax.div(group, 2), 2) == lax.rem(lax.div(row, 2), 2)
    below = gap > planes // 2
    steps = jnp.where(below, planes - gap, gap)
    receiver = jnp.where(gap == 0, 1 - core, jnp.where(below, 0, 1))
    first = jnp.where(steps == 2, jnp.where(same_chip, 4, 2), jnp.where(same_chip, 0, 7))
    place = jnp.where(gap == 0, 6, first + jnp.where(core == receiver, 0, 1))
    slot = 2 + place + jnp.where(receiver == lax.rem(row, 2), 0, 9)
    slot = jnp.where((gap == 0) & same_chip, jnp.where(same_core, 0, 1), slot)
    return slot * blocks + lax.rem(block, blocks)


def adjoint_kernel(
    order_in, cot_in, pre_in, agg_in, w_in, in_in, to_in, out_ref, wpart_ref, place_ref, target_ref,
    order_ref, cot_ref, pre_ref, agg_ref, w_ref, in_ref, to_ref, sems,
):
    ins = (order_in, cot_in, pre_in, w_in, agg_in, in_in, to_in)
    held = (order_ref, cot_ref, pre_ref, w_ref, agg_ref, in_ref, to_ref)
    copies = [pltpu.make_async_copy(a, b, sems.at[i]) for i, (a, b) in enumerate(zip(ins, held))]
    for copy in copies:
        copy.start()
    for copy in copies:
        copy.wait()
    rows = cot_ref.shape[0]
    row, cols, blocks = lax.axis_index("row"), lax.axis_size("col"), rows // SIDE
    place_ref[...] = block_place(in_ref[...], row, lax.axis_size("row") // PLANE, cols, blocks) * SIDE
    target_ref[...] = to_ref[...] - row * cols * blocks
    cot = cot_ref[...]
    row_id = lax.broadcasted_iota(jnp.int32, (rows, SIDE), 0)
    base = (lax.axis_index("row") * lax.axis_size("col") + lax.axis_index("col")) * rows
    total = jnp.zeros(w_ref.shape, F32)
    for b in range(rows // SIDE):
        span = slice(b * SIDE, (b + 1) * SIDE)
        local = order_ref[b : b + 1, :] - base
        pick = jnp.where(row_id == local, 1.0, 0.0).astype(BF)
        grad_rows = dot(pick, cot, (0, 0))
        grad_pre = jnp.where(pre_ref[span, :].astype(F32) > 0, grad_rows, 0.0).astype(BF)
        total += dot(agg_ref[span, :], grad_pre, (0, 0))
        out_ref[span, :] = dot(grad_pre, w_ref[...], (1, 1)).astype(BF)
    for z in range(wpart_ref.shape[0]):
        wpart_ref[z] = total.astype(BF)


def halves_kernel(parts_ref, out_ref):
    total = parts_ref[0].astype(F32)
    for z in range(1, parts_ref.shape[0]):
        total += parts_ref[z].astype(F32)
    high = total.astype(BF)
    out_ref[: total.shape[0], :] = high
    out_ref[total.shape[0] :, :] = (total - high.astype(F32)).astype(BF)


def tile_kernel(
    from_ref, to_ref, tiles_ref, own, beside, ours, theirs, out_ref, weight_ref, blocks_ref, acc_ref, sent_ref, sems
):
    cols, rows, _ = out_ref.shape
    blocks = rows // SIDE
    feat = weight_ref.shape[0]
    sets = ours.shape[0] - 2 * feat
    at = 0
    for piece in (own[...], beside[...], ours[:sets, :], theirs[:sets, :]):
        blocks_ref[at : at + piece.shape[0], :] = piece
        at += piece.shape[0]
    acc_ref[...] = jnp.zeros_like(acc_ref)

    def one(t, carry):
        at = pl.multiple_of(from_ref[0, t], SIDE)
        acc_ref[to_ref[0, t]] += dot(tiles_ref[t], blocks_ref[pl.ds(at, SIDE), :], (1, 0))
        return carry

    lax.fori_loop(0, tiles_ref.shape[0], one, 0, unroll=8)
    copies = [pltpu.make_async_copy(sent_ref.at[c], out_ref.at[c], sems.at[c]) for c in range(cols)]
    for c in range(cols):
        for b in range(blocks):
            sent_ref[c, b * SIDE : (b + 1) * SIDE, :] = acc_ref[c * blocks + b].astype(BF)
        copies[c].start()
    mine, yours = [
        pair[sets : sets + feat, :].astype(F32) + pair[sets + feat :, :].astype(F32) for pair in (ours, theirs)
    ]
    weight_ref[...] = mine + yours
    for c in range(cols):
        copies[c].wait()


def finish_kernel(scale, got_ref, wsum_ref, out_ref, wgrad_ref):
    total = got_ref[0].astype(F32)
    for c in range(1, got_ref.shape[0]):
        total += got_ref[c].astype(F32)
    out_ref[...] = total.astype(BF)
    wgrad_ref[...] = wsum_ref[...] * scale


def vmem():
    return pl.BlockSpec(memory_space=pltpu.VMEM)


def smem():
    return pl.BlockSpec(memory_space=pltpu.SMEM)


def on_device(cotangent, pre_act, aggregated, weight, tile_values, tile_in, tile_out, order):
    row_count = lax.axis_size("row")
    col_count = lax.axis_size("col")
    nodes, feat = cotangent.shape
    blocks_dev = nodes // SIDE
    half = col_count // 2
    params = pltpu.CompilerParams(vmem_limit_bytes=12 << 20)
    small = pltpu.CompilerParams(vmem_limit_bytes=4 << 20)

    tiles = tile_values.shape[0]
    scalars = jax.ShapeDtypeStruct((1, tiles), jnp.int32)
    adjoint, wpart, places, targets = pl.pallas_call(
        adjoint_kernel,
        out_shape=(jax.ShapeDtypeStruct((nodes, feat), BF), jax.ShapeDtypeStruct((half, feat, feat), BF), scalars, scalars),
        in_specs=[pl.BlockSpec(memory_space=pltpu.HBM)] * 7,
        out_specs=(vmem(),) * 4,
        scratch_shapes=[
            pltpu.VMEM((blocks_dev, SIDE), jnp.int32),
            pltpu.VMEM((nodes, feat), BF),
            pltpu.VMEM((nodes, feat), BF),
            pltpu.VMEM((nodes, feat), BF),
            pltpu.VMEM((feat, feat), BF),
            pltpu.VMEM((1, tiles), jnp.int32),
            pltpu.VMEM((1, tiles), jnp.int32),
            pltpu.SemaphoreType.DMA((7,)),
        ],
        compiler_params=pltpu.CompilerParams(vmem_limit_bytes=60 << 20),
        name="adjoint",
    )(order.reshape(blocks_dev, SIDE), cotangent, pre_act, aggregated, weight, tile_in.reshape(1, tiles), tile_out.reshape(1, tiles))

    def swap(value, bit):
        return lax.ppermute(value, "row", [(i, i ^ bit) for i in range(row_count)])

    def to_plane(value, steps, chip_bit, wanted):
        pairs = [(i, ((i ^ chip_bit) + PLANE * (steps if i % 2 == 0 else -steps)) % row_count) for i in range(row_count)]
        return lax.ppermute(value, "row", [pair for pair in pairs if pair[0] % PLANE in wanted])

    beside = swap(adjoint, 1)
    chip = jnp.concatenate([adjoint, beside])
    near = to_plane(chip, 1, 0, (0, 1, 2, 3))
    far = to_plane(chip, 2, 0, (0, 1, 2, 3))
    across_far = to_plane(chip, 2, 2, (1, 2))
    across = swap(jnp.concatenate([beside, near]), 2)

    groups = [list(range(half)), list(range(half, col_count))]
    wz = lax.all_to_all(wpart, "col", 0, 0, axis_index_groups=groups)
    halves = pl.pallas_call(
        halves_kernel,
        out_shape=jax.ShapeDtypeStruct((2 * feat, feat), BF),
        in_specs=[vmem()],
        out_specs=vmem(),
        compiler_params=small,
        name="halves",
    )(wz)

    def partner(value, axis, bit):
        return lax.ppermute(value, axis, [(i, i ^ bit) for i in range(lax.axis_size(axis))])

    received = jnp.concatenate([near, across_far, far, across, halves])
    other = swap(received, 1)

    sends, wsum = pl.pallas_call(
        tile_kernel,
        out_shape=(jax.ShapeDtypeStruct((col_count, nodes, feat), BF), jax.ShapeDtypeStruct((feat, feat), F32)),
        in_specs=[smem(), smem()] + [vmem()] * 5,
        out_specs=(pl.BlockSpec(memory_space=pl.ANY), vmem()),
        scratch_shapes=[
            pltpu.VMEM((20 * nodes, feat), BF),
            pltpu.VMEM((col_count * blocks_dev, SIDE, feat), F32),
            pltpu.VMEM((col_count, nodes, feat), BF),
            pltpu.SemaphoreType.DMA((col_count,)),
        ],
        compiler_params=params,
        cost_estimate=pl.CostEstimate(
            flops=2 * tiles * SIDE * SIDE * feat, bytes_accessed=6 << 20, transcendentals=0
        ),
        name="tiles",
    )(places, targets, tile_values, adjoint, beside, received, other)

    got = lax.all_to_all(sends, "col", 0, 0)
    planes = row_count // PLANE
    for bit in [PLANE << k for k in range((planes - 1).bit_length() - 1)]:
        wsum = wsum + partner(wsum, "row", bit)
    mirrored = [(i, (planes - 1 - i // PLANE) * PLANE + i % PLANE) for i in range(row_count)]
    wsum = wsum + lax.ppermute(wsum, "row", mirrored)
    wsum = wsum + partner(wsum, "row", 2)
    spots = [(r, c) for r in range(row_count) for c in range(col_count)]
    facing = [(r * col_count + c, (r ^ 2) * col_count + (c + half) % col_count) for r, c in spots]
    wsum = wsum + lax.ppermute(wsum, ("row", "col"), facing)
    scale = 1.0 / float(nodes * row_count * col_count) ** 0.5
    node_grad, weight_grad = pl.pallas_call(
        functools.partial(finish_kernel, scale),
        out_shape=(jax.ShapeDtypeStruct((nodes, feat), BF), jax.ShapeDtypeStruct((feat, feat), F32)),
        in_specs=[vmem(), vmem()],
        out_specs=(vmem(), vmem()),
        compiler_params=small,
        name="finish",
    )(got, wsum)
    return (node_grad, weight_grad)


def solution(mesh):
    split = P(("row", "col"))
    return jax.shard_map(
        on_device,
        mesh=mesh,
        in_specs=(split, split, split, P(), split, split, split, split),
        out_specs=(split, P()),
        check_vma=False,
    )
```
